512 devices in a mesh: row: 16 (over z, y_hi), col: 32 (over y_lo, x, core).
Axes of the slice: x: 4, y: 8 (y_hi: 2, y_lo: 4; y = y_hi * 4 + y_lo), z: 8, core: 2. Of those that a mesh axis runs over, the one named last changes fastest.
Arguments:
- grid_input: bfloat16 [256, 256, 1024], P('row', 'col'), may hold values from -6 to 6
- w_qkv: bfloat16 [1024, 1536], replicated, may hold values from -0.1875 to 0.1875
- out_weight: bfloat16 [1024, 512], replicated, may hold values from -0.25 to 0.25
- head_scale: float32 [8], replicated, may hold values from 4 to 16
- cotangent: bfloat16 [256, 256, 1024], P('row', 'col'), may hold values from -16 to 16
Outputs:
- d_input: bfloat16 [256, 256, 1024], P('row', 'col')
The draws below stay inside these ranges and needn't reach their ends.
All inputs are finite; a program needn't handle non-finite values.
Results may differ from the reference program's by a relative error of at most 0.012.
Values may be sent and summed in bfloat16 or wider, within the bound.
A program may use at most 64 MiB of HBM per device.

```python
import math
import jax
import jax.numpy as jnp
from jax import lax

D = 1024
HEADS = 8
HEAD_DIM = 64
RADIUS = 8
TILE_H = 16
TILE_W = 8
H = 256
W = 256


def block_levels(rng, shape, cuts, smallest, high):
    factor_of, own = 1.0, jax.random.fold_in(rng, 6)
    for axis_at, shards_of in cuts:
        steps = jnp.exp(jax.random.uniform(jax.random.fold_in(own, axis_at), (shards_of,), jnp.float32, smallest / len(cuts), high / len(cuts)))
        factor_of = factor_of * jnp.repeat(steps, shape[axis_at] // shards_of).reshape([-1 if axis == axis_at else 1 for axis in range(len(shape))])
    return factor_of


def scatter_about(rng, shape, spread, most, split=(), kind=jnp.bfloat16):
    values = spread * jax.random.normal(rng, shape, jnp.float32)
    if split:
        values = values * block_levels(rng, shape, split, -0.22, 0.18)
    return jnp.clip(values, -most, most).astype(kind)


def setup_inputs(seed: int = 0) -> dict:
    seeds = jax.random.split(jax.random.key(seed), 6)
    grid_input = scatter_about(seeds[0], (H, W, D), 1.0, 6.0, ((0, 16), (1, 32)))
    w_qkv = scatter_about(seeds[1], (D, 3 * HEADS * HEAD_DIM), D ** -0.5, 0.1875)
    out_weight = scatter_about(seeds[2], (D, HEADS * HEAD_DIM), (HEADS * HEAD_DIM) ** -0.5, 0.25)
    head_scale = jnp.clip(jnp.exp(jax.random.uniform(seeds[3], (HEADS,), jnp.float32, math.log(4.0), math.log(16.0))), 4.0, 16.0)
    cotangent = scatter_about(seeds[4], (H, W, D), 4.0, 16.0, ((0, 16), (1, 32)))
    return dict(grid_input=grid_input, w_qkv=w_qkv, out_weight=out_weight, head_scale=head_scale, cotangent=cotangent)


norm_epsilon = 1e-06

def unit_heads(raw_heads, head_scale):
    shaped = raw_heads.reshape(raw_heads.shape[:-1] + (HEADS, HEAD_DIM))
    squares = lax.optimization_barrier(jnp.sum(shaped * shaped, axis=-1, keepdims=True)) + norm_epsilon
    scaled = shaped * jnp.sqrt(head_scale)[:, None] * lax.rsqrt(squares)
    return scaled.reshape(raw_heads.shape)

def unit_heads_back(raw_heads, upstream, head_scale):
    shaped = raw_heads.reshape(raw_heads.shape[:-1] + (HEADS, HEAD_DIM))
    grads = upstream.reshape(shaped.shape)
    squares = lax.optimization_barrier(jnp.sum(shaped * shaped, axis=-1, keepdims=True)) + norm_epsilon
    along_raw = lax.optimization_barrier(jnp.sum(grads * shaped, axis=-1, keepdims=True)) / squares
    result = jnp.sqrt(head_scale)[:, None] * lax.rsqrt(squares) * (grads - shaped * along_raw)
    return result.reshape(raw_heads.shape)

def pair_window(first, second, extent):
    near_enough = jnp.abs(first[:, None] - second[None, :]) <= RADIUS
    inside = (first[:, None] >= 0) & (first[:, None] < extent) & (second[None, :] >= 0) & (second[None, :] < extent)
    return near_enough & inside

def window_mask(query_rows, query_cols, key_rows, key_cols, height, width_grid):
    rows_ok = pair_window(query_rows, key_rows, height)
    cols_ok = pair_window(query_cols, key_cols, width_grid)
    joined = rows_ok[:, None, :, None] & cols_ok[None, :, None, :]
    return joined.reshape(query_rows.shape[0] * query_cols.shape[0], key_rows.shape[0] * key_cols.shape[0])

def attend_block(queries, cotangents, keys, values, window, head_scale):
    count_q = queries.shape[0]
    count_k = keys.shape[0]
    query_heads = queries.astype(jnp.float32).reshape(count_q, HEADS, HEAD_DIM)
    cot_heads = cotangents.astype(jnp.float32).reshape(count_q, HEADS, HEAD_DIM)
    key_heads = keys.astype(jnp.float32).reshape(count_k, HEADS, HEAD_DIM)
    value_heads = values.astype(jnp.float32).reshape(count_k, HEADS, HEAD_DIM)
    scores = jnp.einsum('qhd,khd->hqk', query_heads, key_heads)
    weights = jnp.where(window[None], jnp.exp(scores - head_scale[:, None, None]), 0.0)
    totals = lax.optimization_barrier(jnp.sum(weights, axis=-1, keepdims=True))
    probs = weights / totals
    probs_bf = lax.optimization_barrier(probs.astype(jnp.bfloat16)).astype(jnp.float32)
    attended = jnp.einsum('hqk,khd->hqd', probs_bf, value_heads)
    delta = lax.optimization_barrier(jnp.sum(jnp.transpose(cot_heads, (1, 0, 2)) * attended, axis=-1, keepdims=True))
    dprobs = jnp.einsum('qhd,khd->hqk', cot_heads, value_heads)
    dscore = lax.optimization_barrier((probs * (dprobs - delta)).astype(jnp.bfloat16)).astype(jnp.float32)
    dquery = jnp.einsum('hqk,khd->qhd', dscore, key_heads)
    dkey = jnp.einsum('hqk,qhd->khd', dscore, query_heads)
    dvalue = jnp.einsum('hqk,qhd->khd', probs_bf, cot_heads)
    return (dquery.reshape(count_q, -1), dkey.reshape(count_k, -1), dvalue.reshape(count_k, -1))

def reference(grid_input, w_qkv, out_weight, head_scale, cotangent):
    width_heads = HEADS * HEAD_DIM
    projected = jnp.dot(grid_input.reshape(H * W, D), w_qkv, preferred_element_type=jnp.float32)
    query_raw = projected[:, :width_heads]
    key_raw = projected[:, width_heads:2 * width_heads]
    query_hat = unit_heads(query_raw, head_scale).astype(jnp.bfloat16)
    key_hat = unit_heads(key_raw, head_scale).astype(jnp.bfloat16)
    values = projected[:, 2 * width_heads:].astype(jnp.bfloat16)
    d_att = jnp.dot(cotangent.reshape(H * W, D), out_weight, preferred_element_type=jnp.float32).astype(jnp.bfloat16)
    query_grid = query_hat.reshape(H, W, width_heads)
    cot_grid = d_att.reshape(H, W, width_heads)
    key_value = jnp.concatenate([key_hat, values], axis=-1).reshape(H, W, 2 * width_heads)
    key_value = jnp.pad(key_value, ((RADIUS, RADIUS), (RADIUS, RADIUS), (0, 0)))
    blocks_across = W // TILE_W
    block_count = H // TILE_H * blocks_across
    span_h = TILE_H + 2 * RADIUS
    span_w = TILE_W + 2 * RADIUS
    anchor = jnp.zeros((), jnp.int32)

    def step(accum, block):
        row_start = block // blocks_across * TILE_H
        col_start = block % blocks_across * TILE_W
        queries = lax.dynamic_slice(query_grid, (row_start, col_start, anchor), (TILE_H, TILE_W, width_heads)).reshape(-1, width_heads)
        cots = lax.dynamic_slice(cot_grid, (row_start, col_start, anchor), (TILE_H, TILE_W, width_heads)).reshape(-1, width_heads)
        neighbours = lax.dynamic_slice(key_value, (row_start, col_start, anchor), (span_h, span_w, 2 * width_heads)).reshape(-1, 2 * width_heads)
        window = window_mask(row_start + jnp.arange(TILE_H, dtype=jnp.int32), col_start + jnp.arange(TILE_W, dtype=jnp.int32), row_start - RADIUS + jnp.arange(span_h, dtype=jnp.int32), col_start - RADIUS + jnp.arange(span_w, dtype=jnp.int32), H, W)
        dquery, dkey, dvalue = attend_block(queries, cots, neighbours[:, :width_heads], neighbours[:, width_heads:], window, head_scale)
        update = jnp.concatenate([dkey, dvalue], axis=-1).reshape(span_h, span_w, 2 * width_heads)
        current = lax.dynamic_slice(accum, (row_start, col_start, anchor), (span_h, span_w, 2 * width_heads))
        accum = lax.dynamic_update_slice(accum, current + update.astype(accum.dtype), (row_start, col_start, anchor))
        return (accum, dquery.reshape(TILE_H, TILE_W, width_heads))
    start = jnp.zeros((H + 2 * RADIUS, W + 2 * RADIUS, 2 * width_heads), jnp.float32)
    accum, dquery_blocks = lax.scan(step, start, jnp.arange(block_count, dtype=jnp.int32))
    dquery_hat = dquery_blocks.reshape(H // TILE_H, blocks_across, TILE_H, TILE_W, width_heads)
    dquery_hat = dquery_hat.transpose(0, 2, 1, 3, 4).reshape(H * W, width_heads)
    key_grads = accum[RADIUS:RADIUS + H, RADIUS:RADIUS + W].reshape(H * W, 2 * width_heads)
    dquery = unit_heads_back(query_raw, dquery_hat, head_scale)
    dkey = unit_heads_back(key_raw, key_grads[:, :width_heads], head_scale)
    dqkv = jnp.concatenate([dquery, dkey, key_grads[:, width_heads:]], axis=-1).astype(jnp.bfloat16)
    d_input = jnp.dot(dqkv, w_qkv.T, preferred_element_type=jnp.float32).astype(jnp.bfloat16)
    return d_input.reshape(H, W, D)
```

```python
import jax
import jax.numpy as jnp
from jax import lax
from jax.experimental import pallas as pl
from jax.experimental.pallas import tpu as pltpu
from jax.sharding import PartitionSpec as P

D = 1024
HEADS = 8
HEAD_DIM = 64
RADIUS = 8
PAIRS = HEADS // 2
PAIR = 2 * HEAD_DIM
WIDTH = HEADS * HEAD_DIM
TILE_H = 16
TILE_W = 8
OWN = TILE_H * TILE_W
HALF = OWN // 2
GROUP = 3 * OWN

norm_epsilon = 1e-06

MESH = pl.DeviceIdType.MESH
F32 = jnp.float32
BF16 = jnp.bfloat16
AROUND = [(dr, dc) for dr in (-1, 0, 1) for dc in (-1, 0, 1) if (dr, dc) != (0, 0)]


def slot_of(dr, dc):
    return (dr + 1) * 3 + (dc + 1)


def dot(a, b):
    return lax.dot_general(a, b, (((1,), (0,)), ((), ())), preferred_element_type=F32)


def dot_nt(a, b):
    return lax.dot_general(a, b, (((1,), (1,)), ((), ())), preferred_element_type=F32)


def head_sums(array, ones):
    high = array.astype(BF16)
    low = (array - high.astype(F32)).astype(BF16)
    return dot(high, ones) + dot(low, ones)


def kernel(
    scale_ref, x_hbm, w_hbm, ow_hbm, cot_hbm, out_ref,
    xa, xb, da, db, w, ow, cot,
    qa, ka, va, qb, kb, vb,
    qm, km, vm, dm, qraw, kraw,
    mask_a, mask_b,
    ea, pa, eb, pb, fa, ga, fb, gb,
    zbc, dbc, zmine, znear, za, zb,
    dqkv,
    local_sem, ys, yr, cs, cr, fs, fr, zs, zr,
):
    nrow, ncol = lax.axis_size("row"), lax.axis_size("col")
    r, c = lax.axis_index("row"), lax.axis_index("col")

    def has(dr, dc):
        ok = None
        for at, d, n in ((r, dr, nrow), (c, dc, ncol)):
            if d:
                here = at > 0 if d < 0 else at < n - 1
                ok = here if ok is None else jnp.logical_and(ok, here)
        return ok

    def device(dr, dc):
        return (jnp.clip(r + dr, 0, nrow - 1), jnp.clip(c + dc, 0, ncol - 1))

    def remote(src, dst, send, recv, dr, dc):
        return pltpu.make_async_remote_copy(
            src_ref=src, dst_ref=dst, send_sem=send, recv_sem=recv,
            device_id=device(dr, dc), device_id_type=MESH,
        )

    barrier = pltpu.get_barrier_semaphore()
    count = 0
    for dr, dc in AROUND:
        there = has(dr, dc)
        count = count + there.astype(jnp.int32)

        @pl.when(there)
        def _():
            pl.semaphore_signal(barrier, inc=1, device_id=device(dr, dc), device_id_type=MESH)

    local = [
        pltpu.make_async_copy(src, dst, local_sem.at[i])
        for i, (src, dst) in enumerate(((cot_hbm, cot), (ow_hbm, ow), (x_hbm, xa.at[1]), (w_hbm, w)))
    ]
    for copy in local:
        copy.start()

    def top(n):
        return pl.ds(0, HALF) if n == 0 else pl.ds(HALF, HALF)

    def y_copy(kind, dr):
        src, dst = (x_hbm, xb) if kind == 0 else (da.at[1], db)
        mine, theirs = (0, 1) if dr < 0 else (1, 0)
        i = 2 * kind + (dr > 0)
        return remote(src.at[top(mine)], dst.at[1, top(theirs)], ys.at[i], yr.at[i], dr, 0)

    def c_copy(kind, dc):
        src, dst = (x_hbm, xa) if kind == 0 else (da.at[1], da)
        i = 2 * kind + (dc > 0)
        return remote(src, dst.at[0 if dc > 0 else 2], cs.at[i], cr.at[i], 0, dc)

    def f_copy(kind, half, dc):
        buf = xb if kind == 0 else db
        i = 4 * kind + 2 * half + (dc > 0)
        return remote(
            buf.at[1, top(half)], buf.at[0 if dc > 0 else 2, top(half)], fs.at[i], fr.at[i], 0, dc
        )

    def z_copy(dr, dc):
        i = slot_of(dr, dc)
        return remote(zmine, znear.at[slot_of(-dr, -dc)], zs.at[i], zr.at[i], dr, dc)

    def halo_from(half):
        return has(-1, 0) if half == 0 else has(1, 0)

    pl.semaphore_wait(barrier, count)
    for dr in (-1, 1):

        @pl.when(has(dr, 0))
        def _():
            y_copy(0, dr).start()

    for dc in (-1, 1):

        @pl.when(has(0, dc))
        def _():
            c_copy(0, dc).start()

    for dc in (-1, 1):

        @pl.when(jnp.logical_not(has(0, dc)))
        def _():
            b = 1 + dc
            xa[b] = jnp.zeros((OWN, D), BF16)
            da[b] = jnp.zeros((OWN, WIDTH), BF16)
            xb[b] = jnp.zeros((OWN, D), BF16)
            db[b] = jnp.zeros((OWN, WIDTH), BF16)

    for half in (0, 1):

        @pl.when(jnp.logical_not(halo_from(half)))
        def _():
            for b in range(3):
                xb[b, top(half)] = jnp.zeros((HALF, D), BF16)
                db[b, top(half)] = jnp.zeros((HALF, WIDTH), BF16)

    for dr, dc in AROUND:

        @pl.when(jnp.logical_not(has(dr, dc)))
        def _():
            znear[slot_of(dr, dc)] = jnp.zeros((2 * HEADS, OWN), F32)

    local[0].wait()
    local[1].wait()
    for n in range(2):
        cols = pl.ds(256 * n, 256)
        da[1, :, cols] = dot(cot[...], ow[:, cols]).astype(BF16)
    for dr in (-1, 1):

        @pl.when(has(dr, 0))
        def _():
            y_copy(1, dr).start()

    for dc in (-1, 1):

        @pl.when(has(0, dc))
        def _():
            c_copy(1, dc).start()

    def head_ones(n):
        a = lax.broadcasted_iota(jnp.int32, (n, n), 0) // HEAD_DIM
        b = lax.broadcasted_iota(jnp.int32, (n, n), 1) // HEAD_DIM
        return jnp.where(a == b, 1.0, 0.0).astype(BF16)

    def scale_row(first, heads):
        lane = lax.broadcasted_iota(jnp.int32, (1, heads * HEAD_DIM), 1) // HEAD_DIM
        row = jnp.zeros((1, heads * HEAD_DIM), F32)
        for h in range(heads):
            row = jnp.where(lane == h, scale_ref[first + h], row)
        return jnp.sqrt(row)

    quad_rows = [scale_row(0, 4), scale_row(4, 4)]
    own = lax.broadcasted_iota(jnp.int32, (OWN, GROUP), 0)
    other = lax.broadcasted_iota(jnp.int32, (OWN, GROUP), 1)
    own_i, own_j = own // TILE_W, own % TILE_W
    there_i = (other % OWN) // TILE_W
    there_j = other % TILE_W + TILE_W * (other // OWN - 1)
    col_at = c * TILE_W + there_j
    cols_ok = (jnp.abs(there_j - own_j) <= RADIUS) & (col_at >= 0) & (col_at < ncol * TILE_W)
    mask_a[...] = jnp.where((jnp.abs(there_i - own_i) <= RADIUS) & cols_ok, 1.0, 0.0)
    halo_i = jnp.where(there_i < RADIUS, there_i - RADIUS, there_i - RADIUS + TILE_H)
    row_at = r * TILE_H + halo_i
    rows_ok = (jnp.abs(halo_i - own_i) <= RADIUS) & (row_at >= 0) & (row_at < nrow * TILE_H)
    mask_b[...] = jnp.where(rows_ok & cols_ok, 1.0, 0.0)

    def project(x_block, q_to, k_to, v_to, rows, raw=False):
        ones = head_ones(256)
        for n in range(6):
            cols = pl.ds(256 * n, 256)
            values = dot(x_block[...], w[:, cols])
            kind, quad = n // 2, n % 2
            if kind < 2:
                if raw:
                    keep = qraw if kind == 0 else kraw
                    keep[:, pl.ds(256 * quad, 256)] = values
                squares = head_sums(values * values, ones) + norm_epsilon
                values = values * quad_rows[quad] * lax.rsqrt(squares)
            result = values.astype(BF16)
            to = (q_to, k_to, v_to)[kind]
            to[2 * quad, rows] = result[:, :PAIR]
            to[2 * quad + 1, rows] = result[:, PAIR:]

    local[2].wait()
    local[3].wait()
    project(xa.at[1], qa, ka, va, pl.ds(OWN, OWN), raw=True)
    first_half = lax.broadcasted_iota(jnp.int32, (OWN, PAIR), 1) < HEAD_DIM
    zero = jnp.zeros((OWN, PAIR), BF16)
    for p in range(PAIRS):
        mine = pl.ds(OWN, OWN)
        for to, values in (
            (qm, qa[p, mine]), (km, ka[p, mine]), (vm, va[p, mine]), (dm, da[1, :, pl.ds(PAIR * p, PAIR)]),
        ):
            to[2 * p] = jnp.where(first_half, values, zero)
            to[2 * p + 1] = jnp.where(first_half, zero, values)

    for dc in (-1, 1):

        @pl.when(has(0, -dc))
        def _():
            c_copy(0, dc).wait_recv()

    def project_sides(x_buf, q_to, k_to, v_to):
        def body(i, carry):
            b = 2 * i
            rows = pl.ds(pl.multiple_of(b * OWN, OWN), OWN)
            project(x_buf.at[b], q_to, k_to, v_to, rows)
            return carry

        lax.fori_loop(0, 2, body, 0)

    project_sides(xa, qa, ka, va)

    def query_first(k_of, v_of, mask, e_to, p_to):
        def body(h, carry):
            p = h // 2
            e = jnp.exp(dot_nt(qm[h], k_of[p])) * mask[...]
            e_to[h] = e
            p_to[h] = dot_nt(dm[h], v_of[p])
            return carry

        lax.fori_loop(0, HEADS, body, 0)

    query_first(ka, va, mask_a, ea, pa)

    for dc in (-1, 1):

        @pl.when(has(0, -dc))
        def _():
            c_copy(1, dc).wait_recv()

    def key_first(q_of, d_of, mask, e_to, p_to):
        def body(h, carry):
            p = h // 2
            e_to[h] = jnp.exp(dot_nt(km[h], q_of[p])) * mask[...]
            cols = pl.ds(pl.multiple_of(p * PAIR, PAIR), PAIR)
            for b in range(3):
                p_to[h, :, pl.ds(b * OWN, OWN)] = dot_nt(vm[h], d_of[b, :, cols])
            return carry

        lax.fori_loop(0, HEADS, body, 0)

    key_first(qa, da, mask_a, fa, ga)

    def pass_on(kind):
        for half, dr in ((0, 1), (1, -1)):

            @pl.when(halo_from(half))
            def _():
                y_copy(kind, dr).wait_recv()
                for dc in (-1, 1):

                    @pl.when(has(0, dc))
                    def _():
                        f_copy(kind, half, dc).start()

    def corners(kind):
        for half in (0, 1):
            for dc in (-1, 1):

                @pl.when(jnp.logical_and(halo_from(half), has(0, -dc)))
                def _():
                    f_copy(kind, half, dc).wait_recv()

    pass_on(0)
    project(xb.at[1], qb, kb, vb, pl.ds(OWN, OWN))
    corners(0)
    project_sides(xb, qb, kb, vb)
    query_first(kb, vb, mask_b, eb, pb)

    lane = lax.broadcasted_iota(jnp.int32, (OWN, OWN), 1)

    def totals(h, table):
        z = jnp.sum(ea[h] + eb[h], axis=1, keepdims=True)
        along = jnp.sum(ea[h] * pa[h] + eb[h] * pb[h], axis=1, keepdims=True)
        inverse = 1.0 / z
        delta = along * inverse
        zbc[h] = jnp.broadcast_to(inverse, (OWN, OWN))
        dbc[h] = jnp.broadcast_to(delta, (OWN, OWN))
        table = jnp.where(lane == h, inverse, table)
        return jnp.where(lane == HEADS + h, delta, table)

    table = lax.fori_loop(0, HEADS, totals, jnp.zeros((OWN, OWN), F32))
    zmine[...] = table.T[: 2 * HEADS]
    for dr, dc in AROUND:

        @pl.when(has(dr, dc))
        def _():
            z_copy(dr, dc).start()

    pass_on(1)

    def per_pair(one_head):
        def body(p, carry):
            parts = [one_head(2 * p), one_head(2 * p + 1)]
            for n in range(len(parts[0])):
                kind, _ = parts[0][n]
                dqkv[kind, p] = jnp.where(first_half, parts[0][n][1], parts[1][n][1])
            return carry

        lax.fori_loop(0, PAIRS, body, 0)

    def query_second(h):
        p = h // 2
        result = jnp.zeros((OWN, PAIR), F32)
        inverse = jnp.concatenate([zbc[h]] * 3, axis=1)
        delta = jnp.concatenate([dbc[h]] * 3, axis=1)
        for e, dp, keys in ((ea, pa, ka), (eb, pb, kb)):
            dscore = (e[h] * inverse * (dp[h] - delta)).astype(BF16)
            result = result + dot(dscore, keys[p])
        return [(0, result)]

    per_pair(query_second)

    corners(1)
    key_first(qb, db, mask_b, fb, gb)
    for dr, dc in AROUND:

        @pl.when(has(dr, dc))
        def _():
            z_copy(-dr, -dc).wait_recv()

    znear[slot_of(0, 0)] = zmine[...]
    below = lax.broadcasted_iota(jnp.int32, (2 * HEADS, OWN), 1) < HALF
    for b in range(3):
        cols = pl.ds(b * OWN, OWN)
        za[:, cols] = znear[slot_of(0, b - 1)]
        up, down = znear[slot_of(-1, b - 1)], znear[slot_of(1, b - 1)]
        zb[:, cols] = pltpu.roll(jnp.where(below, down, up), HALF, 1)

    def key_second(h):
        p = h // 2
        dkey = jnp.zeros((OWN, PAIR), F32)
        dvalue = jnp.zeros((OWN, PAIR), F32)
        cols = pl.ds(pl.multiple_of(p * PAIR, PAIR), PAIR)
        for e, dp, queries, cots, table in ((fa, ga, qa, da, za), (fb, gb, qb, db, zb)):
            probs = e[h] * table[pl.ds(h, 1), :]
            dscore = (probs * (dp[h] - table[pl.ds(HEADS + h, 1), :])).astype(BF16)
            dkey = dkey + dot(dscore, queries[p])
            probs_bf = probs.astype(BF16)
            for b in range(3):
                dvalue = dvalue + dot(probs_bf[:, b * OWN : (b + 1) * OWN], cots[b, :, cols])
        return [(1, dkey), (2, dvalue)]

    per_pair(key_second)

    ones = head_ones(PAIR)
    total = jnp.zeros((OWN, D), F32)
    for kind in range(3):
        for p in range(PAIRS):
            grads = dqkv[kind, p]
            cols = pl.ds(PAIR * p, PAIR)
            if kind < 2:
                raw = (qraw if kind == 0 else kraw)[:, cols]
                squares = head_sums(raw * raw, ones) + norm_epsilon
                along = head_sums(grads * raw, ones) / squares
                row = quad_rows[p // 2][:, PAIR * (p % 2) : PAIR * (p % 2 + 1)]
                grads = row * lax.rsqrt(squares) * (grads - raw * along)
            qm[p] = grads.astype(BF16)
        block = jnp.concatenate([qm[p] for p in range(PAIRS)], axis=1)
        total = total + dot_nt(block, w[:, pl.ds(WIDTH * kind, WIDTH)])
    out_ref[...] = total.astype(BF16)

    for kind in (0, 1):
        for dr in (-1, 1):

            @pl.when(has(dr, 0))
            def _():
                y_copy(kind, dr).wait_send()

        for dc in (-1, 1):

            @pl.when(has(0, dc))
            def _():
                c_copy(kind, dc).wait_send()

            for half in (0, 1):

                @pl.when(jnp.logical_and(halo_from(half), has(0, dc)))
                def _():
                    f_copy(kind, half, dc).wait_send()

    for dr, dc in AROUND:

        @pl.when(has(dr, dc))
        def _():
            z_copy(dr, dc).wait_send()


def per_device(grid_input, w_qkv, out_weight, head_scale, cotangent):
    dma = pltpu.SemaphoreType.DMA
    heads_mine = pltpu.VMEM((HEADS, OWN, PAIR), BF16)
    by_pair = pltpu.VMEM((PAIRS, GROUP, PAIR), BF16)
    scores = pltpu.VMEM((HEADS, OWN, GROUP), F32)
    any_space = pl.BlockSpec(memory_space=pl.ANY)
    result = pl.pallas_call(
        kernel,
        out_shape=jax.ShapeDtypeStruct((OWN, D), BF16),
        in_specs=[pl.BlockSpec(memory_space=pltpu.SMEM)] + [any_space] * 4,
        out_specs=pl.BlockSpec(memory_space=pltpu.VMEM),
        scratch_shapes=[
            pltpu.VMEM((3, OWN, D), BF16),
            pltpu.VMEM((3, OWN, D), BF16),
            pltpu.VMEM((3, OWN, WIDTH), BF16),
            pltpu.VMEM((3, OWN, WIDTH), BF16),
            pltpu.VMEM((D, 3 * WIDTH), BF16),
            pltpu.VMEM((D, WIDTH), BF16),
            pltpu.VMEM((OWN, D), BF16),
            *[by_pair] * 6,
            *[heads_mine] * 4,
            pltpu.VMEM((OWN, WIDTH), F32),
            pltpu.VMEM((OWN, WIDTH), F32),
            pltpu.VMEM((OWN, GROUP), F32),
            pltpu.VMEM((OWN, GROUP), F32),
            *[scores] * 8,
            pltpu.VMEM((HEADS, OWN, OWN), F32),
            pltpu.VMEM((HEADS, OWN, OWN), F32),
            pltpu.VMEM((2 * HEADS, OWN), F32),
            pltpu.VMEM((9, 2 * HEADS, OWN), F32),
            pltpu.VMEM((2 * HEADS, GROUP), F32),
            pltpu.VMEM((2 * HEADS, GROUP), F32),
            pltpu.VMEM((3, PAIRS, OWN, PAIR), F32),
            dma((4,)),
            dma((4,)),
            dma((4,)),
            dma((4,)),
            dma((4,)),
            dma((8,)),
            dma((8,)),
            dma((9,)),
            dma((9,)),
        ],
        compiler_params=pltpu.CompilerParams(
            collective_id=0, has_side_effects=True, vmem_limit_bytes=48 << 20
        ),
    )(
        head_scale,
        grid_input.reshape(OWN, D),
        w_qkv,
        out_weight,
        cotangent.reshape(OWN, D),
    )
    return result.reshape(TILE_H, TILE_W, D)


def solution(mesh):
    placed = (P("row", "col", None), P(), P(), P(), P("row", "col", None))
    return jax.shard_map(
        per_device, mesh=mesh, in_specs=placed, out_specs=P("row", "col", None), check_vma=False
    )
```

```python
import jax
import jax.numpy as jnp
from jax import lax
from jax.experimental import pallas as pl
from jax.experimental.pallas import tpu as pltpu
from jax.sharding import PartitionSpec as P

D = 1024
HEADS = 8
HEAD_DIM = 64
RADIUS = 8
PAIRS = HEADS // 2
PAIR = 2 * HEAD_DIM
WIDTH = HEADS * HEAD_DIM
TILE_H = 16
TILE_W = 8
OWN = TILE_H * TILE_W
HALF = OWN // 2
GROUP = 3 * OWN

norm_epsilon = 1e-06

MESH = pl.DeviceIdType.MESH
F32 = jnp.float32
BF16 = jnp.bfloat16
AROUND = [(dr, dc) for dr in (-1, 0, 1) for dc in (-1, 0, 1) if (dr, dc) != (0, 0)]


def slot_of(dr, dc):
    return (dr + 1) * 3 + (dc + 1)


def dot(a, b):
    return lax.dot_general(a, b, (((1,), (0,)), ((), ())), preferred_element_type=F32)


def dot_nt(a, b):
    return lax.dot_general(a, b, (((1,), (1,)), ((), ())), preferred_element_type=F32)


def head_sums(array, ones):
    high = array.astype(BF16)
    low = (array - high.astype(F32)).astype(BF16)
    return dot(high, ones) + dot(low, ones)


def kernel(
    scale_hbm, x_hbm, w_hbm, ow_hbm, cot_hbm, out_ref,
    scale_ref, xa, xb, da, db, w, ow, cot,
    qa, ka, va, qb, kb, vb,
    qm, km, vm, dm, raws, back_own, back_raw,
    mask_a, mask_b,
    ea, pa, eb, pb, fa, ga, fb, gb,
    zpart, apart, zbc, dbc, zmine, znear, za, zb,
    dqkv, partial,
    local_sem, ys, yr, cs, cr, fs, fr, zs, zr,
):
    nrow, ncol = lax.axis_size("row"), lax.axis_size("col")
    r, c = lax.axis_index("row"), lax.axis_index("col")

    def has(dr, dc):
        ok = None
        for at, d, n in ((r, dr, nrow), (c, dc, ncol)):
            if d:
                here = at > 0 if d < 0 else at < n - 1
                ok = here if ok is None else jnp.logical_and(ok, here)
        return ok

    def device(dr, dc):
        return (jnp.clip(r + dr, 0, nrow - 1), jnp.clip(c + dc, 0, ncol - 1))

    def remote(src, dst, send, recv, dr, dc):
        return pltpu.make_async_remote_copy(
            src_ref=src, dst_ref=dst, send_sem=send, recv_sem=recv,
            device_id=device(dr, dc), device_id_type=MESH,
        )

    barrier = pltpu.get_barrier_semaphore()
    count = 0
    for dr, dc in AROUND:
        there = has(dr, dc)
        count = count + there.astype(jnp.int32)

        @pl.when(there)
        def _():
            pl.semaphore_signal(barrier, inc=1, device_id=device(dr, dc), device_id_type=MESH)

    local = [
        pltpu.make_async_copy(src, dst, local_sem.at[i])
        for i, (src, dst) in enumerate(
            ((cot_hbm, cot), (ow_hbm, ow), (x_hbm, xa.at[0]), (w_hbm, w), (scale_hbm, scale_ref))
        )
    ]
    for copy in local:
        copy.start()

    def block_of(dc):
        return 0 if dc == 0 else (1 if dc < 0 else 2)

    def half(n):
        return pl.ds(HALF * n, HALF)

    def y_copy(kind, dr):
        mine = 0 if dr < 0 else 1
        src, dst = (x_hbm, xb.at[0, half(1 - mine)]) if kind == 0 else (da.at[0], db.at[1 - mine, half(0)])
        i = 2 * kind + (dr > 0)
        return remote(src.at[half(mine)], dst, ys.at[i], yr.at[i], dr, 0)

    def c_copy(kind, dc):
        src, dst = (x_hbm, xa) if kind == 0 else (da.at[0], da)
        i = 2 * kind + (dc > 0)
        return remote(src, dst.at[block_of(-dc)], cs.at[i], cr.at[i], 0, dc)

    def f_copy(kind, n, dc):
        i = 4 * kind + 2 * n + (dc > 0)
        b = block_of(-dc)
        if kind == 0:
            src, dst = xb.at[0, half(n)], xb.at[b, half(n)]
        else:
            src, dst = db.at[n, half(0)], db.at[n, half(b)]
        return remote(src, dst, fs.at[i], fr.at[i], 0, dc)

    def z_copy(dr, dc):
        i = slot_of(dr, dc)
        return remote(zmine, znear.at[slot_of(-dr, -dc)], zs.at[i], zr.at[i], dr, dc)

    def halo_from(n):
        return has(-1, 0) if n == 0 else has(1, 0)

    pl.semaphore_wait(barrier, count)
    for dr in (-1, 1):

        @pl.when(has(dr, 0))
        def _():
            y_copy(0, dr).start()

    for dc in (-1, 1):

        @pl.when(has(0, dc))
        def _():
            c_copy(0, dc).start()

    for dc in (-1, 1):

        @pl.when(jnp.logical_not(has(0, dc)))
        def _():
            b = block_of(dc)
            xa[b] = jnp.zeros((OWN, D), BF16)
            da[b] = jnp.zeros((OWN, WIDTH), BF16)
            xb[b] = jnp.zeros((OWN, D), BF16)
            for n in (0, 1):
                db[n, half(b)] = jnp.zeros((HALF, WIDTH), BF16)

    for n in (0, 1):

        @pl.when(jnp.logical_not(halo_from(n)))
        def _():
            for b in range(3):
                xb[b, half(n)] = jnp.zeros((HALF, D), BF16)
            db[n] = jnp.zeros((3 * HALF, WIDTH), BF16)

    for dr, dc in AROUND:

        @pl.when(jnp.logical_not(has(dr, dc)))
        def _():
            znear[slot_of(dr, dc)] = jnp.zeros((2 * HEADS, OWN), F32)

    local[0].wait()
    local[1].wait()
    for n in range(2):
        cols = pl.ds(256 * n, 256)
        da[0, :, cols] = dot(cot[...], ow[:, cols]).astype(BF16)
    for dr in (-1, 1):

        @pl.when(has(dr, 0))
        def _():
            y_copy(1, dr).start()

    for dc in (-1, 1):

        @pl.when(has(0, dc))
        def _():
            c_copy(1, dc).start()

    local[4].wait()
    local[2].wait()
    local[3].wait()

    def head_ones(n):
        a = lax.broadcasted_iota(jnp.int32, (n, n), 0) // HEAD_DIM
        b = lax.broadcasted_iota(jnp.int32, (n, n), 1) // HEAD_DIM
        return jnp.where(a == b, 1.0, 0.0).astype(BF16)

    def scale_row(first, heads):
        lane = lax.broadcasted_iota(jnp.int32, (1, heads * HEAD_DIM), 1) // HEAD_DIM
        row = jnp.zeros((1, heads * HEAD_DIM), F32)
        for h in range(heads):
            row = jnp.where(lane == h, scale_ref[first + h], row)
        return jnp.sqrt(row)

    quad_rows = [scale_row(0, 4), scale_row(4, 4)]
    ones256 = head_ones(256)

    def window(rows, first_half, lanes, block, halo):
        row = lax.broadcasted_iota(jnp.int32, (rows, lanes), 0)
        lane = lax.broadcasted_iota(jnp.int32, (rows, lanes), 1)
        own_i = (row // OWN + first_half) * RADIUS + (row % HALF) // TILE_W
        own_j = row % TILE_W
        b = lane // block
        there_i = (lane % block) // TILE_W
        if halo:
            there_i = there_i - RADIUS if first_half == 0 else there_i + TILE_H
        there_j = lane % TILE_W + jnp.where(b == 0, 0, jnp.where(b == 1, -TILE_W, TILE_W))
        row_at, col_at = r * TILE_H + there_i, c * TILE_W + there_j
        near = (jnp.abs(there_i - own_i) <= RADIUS) & (jnp.abs(there_j - own_j) <= RADIUS)
        inside = (row_at >= 0) & (row_at < nrow * TILE_H) & (col_at >= 0) & (col_at < ncol * TILE_W)
        return jnp.where(near & inside, 1.0, 0.0)

    mask_a[...] = window(2 * OWN, 0, GROUP, OWN, False)
    for n in (0, 1):
        mask_b[n] = window(OWN, n, 3 * HALF, HALF, True)

    def project(x_rows, store, own=False):
        for n in range(6):
            values = dot(x_rows, w[:, pl.ds(256 * n, 256)])
            kind, quad = n // 2, n % 2
            if kind < 2:
                if own:
                    squares = head_sums(values * values, ones256) + norm_epsilon
                    factor = quad_rows[quad] * lax.rsqrt(squares)
                    cols = pl.ds(256 * quad, 256)
                    raws[kind, :, cols] = values
                    back_own[kind, :, cols] = factor
                    back_raw[kind, :, cols] = factor * values / squares
                else:
                    squares = dot((values * values).astype(BF16), ones256) + norm_epsilon
                    factor = quad_rows[quad] * lax.rsqrt(squares)
                values = values * factor
            result = values.astype(BF16)
            store(kind, 2 * quad, result[:, :PAIR])
            store(kind, 2 * quad + 1, result[:, PAIR:])

    def store_a(first):
        def store(kind, p, result):
            (qa, ka, va)[kind][p, pl.ds(first, result.shape[0])] = result

        return store

    def store_b(first):
        def store(kind, p, result):
            to = (qb, kb, vb)[kind]
            for i in range(result.shape[0] // HALF):
                to[i % 2, p, half(first + i // 2)] = result[HALF * i : HALF * (i + 1)]

        return store

    project(xa[0], store_a(0), own=True)
    first_lanes = lax.broadcasted_iota(jnp.int32, (HALF, PAIR), 1) < HEAD_DIM
    zero = jnp.zeros((HALF, PAIR), BF16)
    for p in range(PAIRS):
        for to, values in (
            (qm, qa[p, pl.ds(0, OWN)]), (km, ka[p, pl.ds(0, OWN)]), (vm, va[p, pl.ds(0, OWN)]),
            (dm, da[0, :, pl.ds(PAIR * p, PAIR)]),
        ):
            for n in (0, 1):
                rows = values[HALF * n : HALF * (n + 1)]
                to[p, half(2 * n)] = jnp.where(first_lanes, rows, zero)
                to[p, half(2 * n + 1)] = jnp.where(first_lanes, zero, rows)

    for dc in (-1, 1):

        @pl.when(has(0, -dc))
        def _():
            c_copy(0, dc).wait_recv()

    project(xa[1:3].reshape(2 * OWN, D), store_a(OWN))

    def tiles(array):
        return array[:, :OWN] + array[:, OWN : 2 * OWN] + array[:, 2 * OWN :]

    def query_a(p, carry):
        e = jnp.exp(dot_nt(qm[p], ka[p])) * mask_a[...]
        dp = dot_nt(dm[p], va[p])
        ea[p] = e
        pa[p] = dp
        zpart[p] = tiles(e)
        apart[p] = tiles(e * dp)
        return carry

    lax.fori_loop(0, PAIRS, query_a, 0)

    def pass_on(kind):
        for n, dr in ((0, 1), (1, -1)):

            @pl.when(halo_from(n))
            def _():
                y_copy(kind, dr).wait_recv()
                for dc in (-1, 1):

                    @pl.when(has(0, dc))
                    def _():
                        f_copy(kind, n, dc).start()

    def corners(kind):
        for n in (0, 1):
            for dc in (-1, 1):

                @pl.when(jnp.logical_and(halo_from(n), has(0, -dc)))
                def _():
                    f_copy(kind, n, dc).wait_recv()

    pass_on(0)
    project(xb[0], store_b(0))

    for dc in (-1, 1):

        @pl.when(has(0, -dc))
        def _():
            c_copy(1, dc).wait_recv()

    def lanes_of(p):
        return pl.ds(pl.multiple_of(p * PAIR, PAIR), PAIR)

    def key_a(p, carry):
        fa[p] = jnp.exp(dot_nt(km[p], qa[p])) * mask_a[...]
        ga[p] = dot_nt(vm[p], da[:, :, lanes_of(p)].reshape(GROUP, PAIR))
        return carry

    lax.fori_loop(0, PAIRS, key_a, 0)

    corners(0)
    project(xb[1:3].reshape(2 * OWN, D), store_b(1))
    pass_on(1)

    lane = lax.broadcasted_iota(jnp.int32, (2 * OWN, OWN), 1)

    def query_b(p, table):
        z, along = [], []
        for n in (0, 1):
            rows = pl.ds(OWN * n, OWN)
            e = jnp.exp(dot_nt(qm[p, rows], kb[n, p])) * mask_b[n]
            dp = dot_nt(dm[p, rows], vb[n, p])
            eb[p, n] = e
            pb[p, n] = dp
            z.append(jnp.sum(e, axis=1, keepdims=True))
            along.append(jnp.sum(e * dp, axis=1, keepdims=True))
        z = jnp.concatenate(z, axis=0) + jnp.sum(zpart[p], axis=1, keepdims=True)
        along = jnp.concatenate(along, axis=0) + jnp.sum(apart[p], axis=1, keepdims=True)
        inverse = 1.0 / z
        delta = along * inverse
        zbc[p] = jnp.broadcast_to(inverse, (2 * OWN, OWN))
        dbc[p] = jnp.broadcast_to(delta, (2 * OWN, OWN))
        table = jnp.where(lane == p, inverse, table)
        return jnp.where(lane == PAIRS + p, delta, table)

    table = lax.fori_loop(0, PAIRS, query_b, jnp.zeros((2 * OWN, OWN), F32))
    upper, lower = table[:OWN].T[:HEADS], table[OWN:].T[:HEADS]
    left_lanes = lax.broadcasted_iota(jnp.int32, (HEADS, OWN), 1) < HALF
    zmine[pl.ds(0, HEADS)] = jnp.where(left_lanes, upper, pltpu.roll(lower, HALF, 1))
    zmine[pl.ds(HEADS, HEADS)] = jnp.where(left_lanes, pltpu.roll(upper, HALF, 1), lower)
    for dr, dc in AROUND:

        @pl.when(has(dr, dc))
        def _():
            z_copy(dr, dc).start()

    def key_b(p, carry):
        for n in (0, 1):
            fb[p, n] = jnp.exp(dot_nt(km[p, pl.ds(OWN * n, OWN)], qb[n, p])) * mask_b[n]
        return carry

    lax.fori_loop(0, PAIRS, key_b, 0)

    def by_heads(array):
        parts = [array[HALF * i : HALF * (i + 1)] for i in range(4)]
        return jnp.concatenate(
            [jnp.where(first_lanes, parts[2 * n], parts[2 * n + 1]) for n in (0, 1)], axis=0
        )

    def query_second(p, carry):
        inverse, delta = zbc[p], dbc[p]
        wide = jnp.concatenate([inverse] * 3, axis=1)
        dscore = ea[p] * wide * (pa[p] - jnp.concatenate([delta] * 3, axis=1))
        result = dot(dscore.astype(BF16), ka[p])
        more = []
        for n in (0, 1):
            rows = slice(OWN * n, OWN * (n + 1))
            i2 = jnp.concatenate([inverse[rows], inverse[rows, :HALF]], axis=1)
            d2 = jnp.concatenate([delta[rows], delta[rows, :HALF]], axis=1)
            dscore = eb[p, n] * i2 * (pb[p, n] - d2)
            more.append(dot(dscore.astype(BF16), kb[n, p]))
        dqkv[0, p] = by_heads(result + jnp.concatenate(more, axis=0))
        return carry

    lax.fori_loop(0, PAIRS, query_second, 0)
    ones128 = head_ones(PAIR)

    def through_norm(kind):
        blocks = []
        for p in range(PAIRS):
            grads = dqkv[kind, p]
            cols = pl.ds(PAIR * p, PAIR)
            along = head_sums(grads * raws[kind, :, cols], ones128)
            blocks.append(
                (back_own[kind, :, cols] * grads - back_raw[kind, :, cols] * along).astype(BF16)
            )
        return jnp.concatenate(blocks, axis=1)

    partial[...] = dot_nt(through_norm(0), w[:, pl.ds(0, WIDTH)])

    corners(1)

    def key_b_cot(p, carry):
        for n in (0, 1):
            gb[p, n] = dot_nt(vm[p, pl.ds(OWN * n, OWN)], db[n, :, lanes_of(p)])
        return carry

    lax.fori_loop(0, PAIRS, key_b_cot, 0)

    for dr, dc in AROUND:

        @pl.when(has(dr, dc))
        def _():
            z_copy(-dr, -dc).wait_recv()

    znear[slot_of(0, 0)] = zmine[...]
    near_lanes = lax.broadcasted_iota(jnp.int32, (2 * HEADS, OWN), 1) < HALF
    for b, dc in enumerate((0, -1, 1)):
        za[:, pl.ds(b * OWN, OWN)] = znear[slot_of(0, dc)]
    own_up, left_up, right_up = (znear[slot_of(-1, dc)] for dc in (0, -1, 1))
    zb[0, :, pl.ds(0, OWN)] = jnp.where(near_lanes, pltpu.roll(own_up, HALF, 1), left_up)
    zb[0, :, pl.ds(OWN, HALF)] = pltpu.roll(right_up, HALF, 1)[:, :HALF]
    own_down, left_down, right_down = (znear[slot_of(1, dc)] for dc in (0, -1, 1))
    zb[1, :, pl.ds(0, OWN)] = jnp.where(near_lanes, own_down, pltpu.roll(left_down, HALF, 1))
    zb[1, :, pl.ds(OWN, HALF)] = right_down[:, :HALF]

    def terms(e, dp, table, p, halves):
        probs, dscore = [], []
        for i in range(2 * halves):
            rows = slice(HALF * i, HALF * (i + 1))
            first = HEADS * (i % 2)
            prob = e[rows] * table[pl.ds(first + p, 1), :]
            probs.append(prob.astype(BF16))
            dscore.append((prob * (dp[rows] - table[pl.ds(first + PAIRS + p, 1), :])).astype(BF16))
        return jnp.concatenate(probs, axis=0), jnp.concatenate(dscore, axis=0)

    def key_second(p, carry):
        probs, dscore = terms(fa[p], ga[p], za, p, 2)
        dkey = dot(dscore, qa[p])
        dvalue = dot(probs, da[:, :, lanes_of(p)].reshape(GROUP, PAIR))
        more_k, more_v = [], []
        for n in (0, 1):
            probs, dscore = terms(fb[p, n], gb[p, n], zb.at[n], p, 1)
            more_k.append(dot(dscore, qb[n, p]))
            more_v.append(dot(probs, db[n, :, lanes_of(p)]))
        dqkv[1, p] = by_heads(dkey + jnp.concatenate(more_k, axis=0))
        dqkv[2, p] = by_heads(dvalue + jnp.concatenate(more_v, axis=0))
        return carry

    lax.fori_loop(0, PAIRS, key_second, 0)

    dvalues = jnp.concatenate([dqkv[2, p].astype(BF16) for p in range(PAIRS)], axis=1)
    total = partial[...] + dot_nt(dvalues, w[:, pl.ds(2 * WIDTH, WIDTH)])
    total = total + dot_nt(through_norm(1), w[:, pl.ds(WIDTH, WIDTH)])
    out_ref[...] = total.astype(BF16)

    for kind in (0, 1):
        for dr in (-1, 1):

            @pl.when(has(dr, 0))
            def _():
                y_copy(kind, dr).wait_send()

        for dc in (-1, 1):

            @pl.when(has(0, dc))
            def _():
                c_copy(kind, dc).wait_send()

            for n in (0, 1):

                @pl.when(jnp.logical_and(halo_from(n), has(0, dc)))
                def _():
                    f_copy(kind, n, dc).wait_send()

    for dr, dc in AROUND:

        @pl.when(has(dr, dc))
        def _():
            z_copy(dr, dc).wait_send()


def per_device(grid_input, w_qkv, out_weight, head_scale, cotangent):
    dma = pltpu.SemaphoreType.DMA
    masked = pltpu.VMEM((PAIRS, 2 * OWN, PAIR), BF16)
    by_pair = pltpu.VMEM((PAIRS, GROUP, PAIR), BF16)
    halo_by_pair = pltpu.VMEM((2, PAIRS, 3 * HALF, PAIR), BF16)
    scores = pltpu.VMEM((PAIRS, 2 * OWN, GROUP), F32)
    halo_scores = pltpu.VMEM((PAIRS, 2, OWN, 3 * HALF), F32)
    by_query = pltpu.VMEM((PAIRS, 2 * OWN, OWN), F32)
    hbm = pl.BlockSpec(memory_space=pltpu.HBM)
    result = pl.pallas_call(
        kernel,
        out_shape=jax.ShapeDtypeStruct((OWN, D), BF16),
        in_specs=[hbm] * 5,
        out_specs=pl.BlockSpec(memory_space=pltpu.VMEM),
        scratch_shapes=[
            pltpu.SMEM((HEADS,), F32),
            pltpu.VMEM((3, OWN, D), BF16),
            pltpu.VMEM((3, OWN, D), BF16),
            pltpu.VMEM((3, OWN, WIDTH), BF16),
            pltpu.VMEM((2, 3 * HALF, WIDTH), BF16),
            pltpu.VMEM((D, 3 * WIDTH), BF16),
            pltpu.VMEM((D, WIDTH), BF16),
            pltpu.VMEM((OWN, D), BF16),
            *[by_pair] * 3,
            *[halo_by_pair] * 3,
            *[masked] * 4,
            *[pltpu.VMEM((2, OWN, WIDTH), F32)] * 3,
            pltpu.VMEM((2 * OWN, GROUP), F32),
            pltpu.VMEM((2, OWN, 3 * HALF), F32),
            *[scores] * 2,
            *[halo_scores] * 2,
            *[scores] * 2,
            *[halo_scores] * 2,
            *[by_query] * 4,
            pltpu.VMEM((2 * HEADS, OWN), F32),
            pltpu.VMEM((9, 2 * HEADS, OWN), F32),
            pltpu.VMEM((2 * HEADS, GROUP), F32),
            pltpu.VMEM((2, 2 * HEADS, 3 * HALF), F32),
            pltpu.VMEM((3, PAIRS, OWN, PAIR), F32),
            pltpu.VMEM((OWN, D), F32),
            dma((5,)),
            dma((4,)),
            dma((4,)),
            dma((4,)),
            dma((4,)),
            dma((8,)),
            dma((8,)),
            dma((9,)),
            dma((9,)),
        ],
        compiler_params=pltpu.CompilerParams(
            collective_id=0, has_side_effects=True, vmem_limit_bytes=60 << 20
        ),
    )(
        head_scale,
        grid_input.reshape(OWN, D),
        w_qkv,
        out_weight,
        cotangent.reshape(OWN, D),
    )
    return result.reshape(TILE_H, TILE_W, D)


def solution(mesh):
    placed = (P("row", "col", None), P(), P(), P(), P("row", "col", None))
    return jax.shard_map(
        per_device, mesh=mesh, in_specs=placed, out_specs=P("row", "col", None), check_vma=False
    )
```

```python
import jax
import jax.numpy as jnp
from jax import lax
from jax.experimental import pallas as pl
from jax.experimental.pallas import tpu as pltpu
from jax.sharding import PartitionSpec as P

D = 1024
HEADS = 8
HEAD_DIM = 64
RADIUS = 8
PAIRS = HEADS // 2
PAIR = 2 * HEAD_DIM
WIDTH = HEADS * HEAD_DIM
TILE_H = 16
TILE_W = 8
OWN = TILE_H * TILE_W
HALF = OWN // 2
GROUP = 3 * OWN

norm_epsilon = 1e-06

MESH = pl.DeviceIdType.MESH
F32 = jnp.float32
BF16 = jnp.bfloat16
AROUND = [(dr, dc) for dr in (-1, 0, 1) for dc in (-1, 0, 1) if (dr, dc) != (0, 0)]


def slot_of(dr, dc):
    return (dr + 1) * 3 + (dc + 1)


def dot(a, b):
    return lax.dot_general(a, b, (((1,), (0,)), ((), ())), preferred_element_type=F32)


def dot_nt(a, b):
    return lax.dot_general(a, b, (((1,), (1,)), ((), ())), preferred_element_type=F32)


def head_sums(array, ones):
    high = array.astype(BF16)
    low = (array - high.astype(F32)).astype(BF16)
    return dot(high, ones) + dot(low, ones)


def kernel(
    scale_hbm, x_hbm, w_hbm, ow_hbm, cot_hbm, out_ref,
    scale_ref, xa, xb, da, db, w, ow, cot,
    qa, ka, va, qb, kb, vb,
    qm, km, vm, dm, raws, back_own, back_raw,
    mask_a, mask_c, mask_s,
    ea, pa, fa, ga, ec, pc, fc, gc, es, ps, fsd, gs,
    zpart, apart, zbc, dbc, zmine, znear, za, zc, zside,
    dqkv, partial,
    local_sem, ys, yr, cs, cr, fs, fr, zs, zr,
):
    nrow, ncol = lax.axis_size("row"), lax.axis_size("col")
    r, c = lax.axis_index("row"), lax.axis_index("col")

    def has(dr, dc):
        ok = None
        for at, d, n in ((r, dr, nrow), (c, dc, ncol)):
            if d:
                here = at > 0 if d < 0 else at < n - 1
                ok = here if ok is None else jnp.logical_and(ok, here)
        return ok

    def device(dr, dc):
        return (jnp.clip(r + dr, 0, nrow - 1), jnp.clip(c + dc, 0, ncol - 1))

    def remote(src, dst, send, recv, dr, dc):
        return pltpu.make_async_remote_copy(
            src_ref=src, dst_ref=dst, send_sem=send, recv_sem=recv,
            device_id=device(dr, dc), device_id_type=MESH,
        )

    barrier = pltpu.get_barrier_semaphore()
    count = 0
    for dr, dc in AROUND:
        there = has(dr, dc)
        count = count + there.astype(jnp.int32)

        @pl.when(there)
        def _():
            pl.semaphore_signal(barrier, inc=1, device_id=device(dr, dc), device_id_type=MESH)

    local = [
        pltpu.make_async_copy(src, dst, local_sem.at[i])
        for i, (src, dst) in enumerate(
            ((cot_hbm, cot), (ow_hbm, ow), (x_hbm, xa.at[0]), (w_hbm, w), (scale_hbm, scale_ref))
        )
    ]
    for copy in local:
        copy.start()

    def block_of(dc):
        return 0 if dc == 0 else (1 if dc < 0 else 2)

    def half(n):
        return pl.ds(HALF * n, HALF)

    def y_copy(kind, dr):
        mine = 0 if dr < 0 else 1
        src, dst = (x_hbm, xb.at[0, half(1 - mine)]) if kind == 0 else (da.at[0], db.at[1 - mine, half(0)])
        i = 2 * kind + (dr > 0)
        return remote(src.at[half(mine)], dst, ys.at[i], yr.at[i], dr, 0)

    def c_copy(kind, dc):
        src, dst = (x_hbm, xa) if kind == 0 else (da.at[0], da)
        i = 2 * kind + (dc > 0)
        return remote(src, dst.at[block_of(-dc)], cs.at[i], cr.at[i], 0, dc)

    def f_copy(kind, n, dc):
        i = 4 * kind + 2 * n + (dc > 0)
        b = block_of(-dc)
        if kind == 0:
            src, dst = xb.at[0, half(n)], xb.at[b, half(n)]
        else:
            src, dst = db.at[n, half(0)], db.at[n, half(b)]
        return remote(src, dst, fs.at[i], fr.at[i], 0, dc)

    def z_copy(dr, dc):
        i = slot_of(dr, dc)
        return remote(zmine, znear.at[slot_of(-dr, -dc)], zs.at[i], zr.at[i], dr, dc)

    def halo_from(n):
        return has(-1, 0) if n == 0 else has(1, 0)

    pl.semaphore_wait(barrier, count)
    for dr in (-1, 1):

        @pl.when(has(dr, 0))
        def _():
            y_copy(0, dr).start()

    for dc in (-1, 1):

        @pl.when(has(0, dc))
        def _():
            c_copy(0, dc).start()

    for dc in (-1, 1):

        @pl.when(jnp.logical_not(has(0, dc)))
        def _():
            b = block_of(dc)
            xa[b] = jnp.zeros((OWN, D), BF16)
            da[b] = jnp.zeros((OWN, WIDTH), BF16)
            xb[b] = jnp.zeros((OWN, D), BF16)
            for n in (0, 1):
                db[n, half(b)] = jnp.zeros((HALF, WIDTH), BF16)

    for n in (0, 1):

        @pl.when(jnp.logical_not(halo_from(n)))
        def _():
            for b in range(3):
                xb[b, half(n)] = jnp.zeros((HALF, D), BF16)
            db[n] = jnp.zeros((3 * HALF, WIDTH), BF16)

    for dr, dc in AROUND:

        @pl.when(jnp.logical_not(has(dr, dc)))
        def _():
            znear[slot_of(dr, dc)] = jnp.zeros((2 * HEADS, OWN), F32)

    local[0].wait()
    local[1].wait()
    for n in range(2):
        cols = pl.ds(256 * n, 256)
        da[0, :, cols] = dot(cot[...], ow[:, cols]).astype(BF16)
    for dr in (-1, 1):

        @pl.when(has(dr, 0))
        def _():
            y_copy(1, dr).start()

    for dc in (-1, 1):

        @pl.when(has(0, dc))
        def _():
            c_copy(1, dc).start()

    local[4].wait()
    local[2].wait()
    local[3].wait()

    def head_ones(n):
        a = lax.broadcasted_iota(jnp.int32, (n, n), 0) // HEAD_DIM
        b = lax.broadcasted_iota(jnp.int32, (n, n), 1) // HEAD_DIM
        return jnp.where(a == b, 1.0, 0.0).astype(BF16)

    def scale_row(first, heads):
        lane = lax.broadcasted_iota(jnp.int32, (1, heads * HEAD_DIM), 1) // HEAD_DIM
        row = jnp.zeros((1, heads * HEAD_DIM), F32)
        for h in range(heads):
            row = jnp.where(lane == h, scale_ref[first + h], row)
        return jnp.sqrt(row)

    quad_rows = [scale_row(0, 4), scale_row(4, 4)]
    ones256 = head_ones(256)

    def window(rows, first_half, lanes, block, halo, first_block):
        row = lax.broadcasted_iota(jnp.int32, (rows, lanes), 0)
        lane = lax.broadcasted_iota(jnp.int32, (rows, lanes), 1)
        own_i = (row // OWN + first_half) * RADIUS + (row % HALF) // TILE_W
        own_j = row % TILE_W
        b = lane // block + first_block
        there_i = (lane % block) // TILE_W
        if halo:
            there_i = there_i - RADIUS if first_half == 0 else there_i + TILE_H
        there_j = lane % TILE_W + jnp.where(b == 0, 0, jnp.where(b == 1, -TILE_W, TILE_W))
        row_at, col_at = r * TILE_H + there_i, c * TILE_W + there_j
        near = (jnp.abs(there_i - own_i) <= RADIUS) & (jnp.abs(there_j - own_j) <= RADIUS)
        inside = (row_at >= 0) & (row_at < nrow * TILE_H) & (col_at >= 0) & (col_at < ncol * TILE_W)
        return jnp.where(near & inside, 1.0, 0.0)

    mask_a[...] = window(2 * OWN, 0, GROUP, OWN, False, 0)
    for n in (0, 1):
        mask_c[n] = window(OWN, n, HALF, HALF, True, 0)
        mask_s[n] = window(OWN, n, OWN, HALF, True, 1)

    def project(x_rows, store, own=False, chunks=range(6)):
        for n in chunks:
            values = dot(x_rows, w[:, pl.ds(256 * n, 256)])
            kind, quad = n // 2, n % 2
            if kind < 2:
                if own:
                    squares = head_sums(values * values, ones256) + norm_epsilon
                    factor = quad_rows[quad] * lax.rsqrt(squares)
                    cols = pl.ds(256 * quad, 256)
                    raws[kind, :, cols] = values
                    back_own[kind, :, cols] = factor
                    back_raw[kind, :, cols] = factor * values / squares
                else:
                    squares = dot((values * values).astype(BF16), ones256) + norm_epsilon
                    factor = quad_rows[quad] * lax.rsqrt(squares)
                values = values * factor
            result = values.astype(BF16)
            store(kind, 2 * quad, result[:, :PAIR])
            store(kind, 2 * quad + 1, result[:, PAIR:])

    def store_a(first):
        def store(kind, p, result):
            (qa, ka, va)[kind][p, pl.ds(first, result.shape[0])] = result

        return store

    def store_b(first):
        def store(kind, p, result):
            to = (qb, kb, vb)[kind]
            for i in range(result.shape[0] // HALF):
                to[i % 2, p, half(first + i // 2)] = result[HALF * i : HALF * (i + 1)]

        return store

    project(xa[0], store_a(0), own=True)
    first_lanes = lax.broadcasted_iota(jnp.int32, (HALF, PAIR), 1) < HEAD_DIM
    zero = jnp.zeros((HALF, PAIR), BF16)
    for p in range(PAIRS):
        for to, values in (
            (qm, qa[p, pl.ds(0, OWN)]), (km, ka[p, pl.ds(0, OWN)]), (vm, va[p, pl.ds(0, OWN)]),
            (dm, da[0, :, pl.ds(PAIR * p, PAIR)]),
        ):
            for n in (0, 1):
                rows = values[HALF * n : HALF * (n + 1)]
                to[p, half(2 * n)] = jnp.where(first_lanes, rows, zero)
                to[p, half(2 * n + 1)] = jnp.where(first_lanes, zero, rows)

    for dc in (-1, 1):

        @pl.when(has(0, -dc))
        def _():
            c_copy(0, dc).wait_recv()

    project(xa[1:3].reshape(2 * OWN, D), store_a(OWN))

    def tiles(array):
        return array[:, :OWN] + array[:, OWN : 2 * OWN] + array[:, 2 * OWN :]

    def query_a(p, carry):
        e = jnp.exp(dot_nt(qm[p], ka[p])) * mask_a[...]
        dp = dot_nt(dm[p], va[p])
        ea[p] = e
        pa[p] = dp
        zpart[p] = tiles(e)
        apart[p] = tiles(e * dp)
        return carry

    lax.fori_loop(0, PAIRS, query_a, 0, unroll=True)

    def pass_on(kind):
        for n, dr in ((0, 1), (1, -1)):

            @pl.when(halo_from(n))
            def _():
                y_copy(kind, dr).wait_recv()
                for dc in (-1, 1):

                    @pl.when(has(0, dc))
                    def _():
                        f_copy(kind, n, dc).start()

    def corners(kind):
        for n in (0, 1):
            for dc in (-1, 1):

                @pl.when(jnp.logical_and(halo_from(n), has(0, -dc)))
                def _():
                    f_copy(kind, n, dc).wait_recv()

    def lanes_of(p):
        return pl.ds(pl.multiple_of(p * PAIR, PAIR), PAIR)

    NEAR, SIDE = pl.ds(0, HALF), pl.ds(HALF, OWN)

    def rows_of(n):
        return pl.ds(OWN * n, OWN)

    def each_pair(body):
        lax.fori_loop(0, PAIRS, body, 0, unroll=True)

    pass_on(0)
    project(xb[0], store_b(0))

    def near_scores(p, carry):
        z, along = [], []
        for n in (0, 1):
            e = jnp.exp(dot_nt(qm[p, rows_of(n)], kb[n, p, NEAR])) * mask_c[n]
            dp = dot_nt(dm[p, rows_of(n)], vb[n, p, NEAR])
            ec[p, n] = e
            pc[p, n] = dp
            fc[p, n] = jnp.exp(dot_nt(km[p, rows_of(n)], qb[n, p, NEAR])) * mask_c[n]
            z.append(e)
            along.append(e * dp)
        zpart[p, :, NEAR] = zpart[p, :, NEAR] + jnp.concatenate(z, axis=0)
        apart[p, :, NEAR] = apart[p, :, NEAR] + jnp.concatenate(along, axis=0)
        return carry

    each_pair(near_scores)

    for dc in (-1, 1):

        @pl.when(has(0, -dc))
        def _():
            c_copy(1, dc).wait_recv()

    def key_a(p, carry):
        fa[p] = jnp.exp(dot_nt(km[p], qa[p])) * mask_a[...]
        ga[p] = dot_nt(vm[p], da[:, :, lanes_of(p)].reshape(GROUP, PAIR))
        return carry

    each_pair(key_a)

    pass_on(1)
    corners(0)
    x_sides = xb[1:3].reshape(2 * OWN, D)
    project(x_sides, store_b(1), chunks=range(2, 6))

    lane = lax.broadcasted_iota(jnp.int32, (2 * OWN, OWN), 1)

    def side_scores(p, table):
        z, along = [], []
        for n in (0, 1):
            e = jnp.exp(dot_nt(qm[p, rows_of(n)], kb[n, p, SIDE])) * mask_s[n]
            dp = dot_nt(dm[p, rows_of(n)], vb[n, p, SIDE])
            es[p, n] = e
            ps[p, n] = dp
            z.append(e)
            along.append(e * dp)
        z = jnp.sum(jnp.concatenate(z, axis=0) + zpart[p], axis=1, keepdims=True)
        along = jnp.sum(jnp.concatenate(along, axis=0) + apart[p], axis=1, keepdims=True)
        inverse = 1.0 / z
        delta = along * inverse
        zbc[p] = jnp.broadcast_to(inverse, (2 * OWN, OWN))
        dbc[p] = jnp.broadcast_to(delta, (2 * OWN, OWN))
        table = jnp.where(lane == p, inverse, table)
        return jnp.where(lane == PAIRS + p, delta, table)

    table = lax.fori_loop(0, PAIRS, side_scores, jnp.zeros((2 * OWN, OWN), F32), unroll=True)
    upper, lower = table[:OWN].T[:HEADS], table[OWN:].T[:HEADS]
    left_lanes = lax.broadcasted_iota(jnp.int32, (HEADS, OWN), 1) < HALF
    zmine[pl.ds(0, HEADS)] = jnp.where(left_lanes, upper, pltpu.roll(lower, HALF, 1))
    zmine[pl.ds(HEADS, HEADS)] = jnp.where(left_lanes, pltpu.roll(upper, HALF, 1), lower)
    for dr, dc in AROUND:

        @pl.when(has(dr, dc))
        def _():
            z_copy(dr, dc).start()


    project(x_sides, store_b(1), chunks=range(2))

    def key_sides(p, carry):
        for n in (0, 1):
            fsd[p, n] = jnp.exp(dot_nt(km[p, rows_of(n)], qb[n, p, SIDE])) * mask_s[n]
        return carry

    each_pair(key_sides)

    def by_heads(array):
        parts = [array[HALF * i : HALF * (i + 1)] for i in range(4)]
        return jnp.concatenate(
            [jnp.where(first_lanes, parts[2 * n], parts[2 * n + 1]) for n in (0, 1)], axis=0
        )

    def query_second(p, carry):
        inverse, delta = zbc[p], dbc[p]
        wide = jnp.concatenate([inverse] * 3, axis=1)
        dscore = ea[p] * wide * (pa[p] - jnp.concatenate([delta] * 3, axis=1))
        result = dot(dscore.astype(BF16), ka[p])
        more = []
        for n in (0, 1):
            rows = slice(OWN * n, OWN * (n + 1))
            dscore = ec[p, n] * inverse[rows, :HALF] * (pc[p, n] - delta[rows, :HALF])
            near = dot(dscore.astype(BF16), kb[n, p, NEAR])
            dscore = es[p, n] * inverse[rows] * (ps[p, n] - delta[rows])
            more.append(near + dot(dscore.astype(BF16), kb[n, p, SIDE]))
        dqkv[0, p] = by_heads(result + jnp.concatenate(more, axis=0))
        return carry

    each_pair(query_second)
    ones128 = head_ones(PAIR)

    def through_norm(kind):
        blocks = []
        for p in range(PAIRS):
            grads = dqkv[kind, p]
            cols = pl.ds(PAIR * p, PAIR)
            along = head_sums(grads * raws[kind, :, cols], ones128)
            blocks.append(
                (back_own[kind, :, cols] * grads - back_raw[kind, :, cols] * along).astype(BF16)
            )
        return jnp.concatenate(blocks, axis=1)

    partial[...] = dot_nt(through_norm(0), w[:, pl.ds(0, WIDTH)])

    corners(1)

    def key_halo_cot(p, carry):
        for n in (0, 1):
            gc[p, n] = dot_nt(vm[p, rows_of(n)], db[n, NEAR, lanes_of(p)])
            gs[p, n] = dot_nt(vm[p, rows_of(n)], db[n, SIDE, lanes_of(p)])
        return carry

    each_pair(key_halo_cot)

    for dr, dc in AROUND:

        @pl.when(has(dr, dc))
        def _():
            z_copy(-dr, -dc).wait_recv()

    znear[slot_of(0, 0)] = zmine[...]
    near_lanes = lax.broadcasted_iota(jnp.int32, (2 * HEADS, OWN), 1) < HALF
    for b, dc in enumerate((0, -1, 1)):
        za[:, pl.ds(b * OWN, OWN)] = znear[slot_of(0, dc)]
    own_up, left_up, right_up = (znear[slot_of(-1, dc)] for dc in (0, -1, 1))
    zc[0] = pltpu.roll(own_up, HALF, 1)[:, :HALF]
    zside[0] = jnp.where(near_lanes, pltpu.roll(left_up, HALF, 1), right_up)
    own_down, left_down, right_down = (znear[slot_of(1, dc)] for dc in (0, -1, 1))
    zc[1] = own_down[:, :HALF]
    zside[1] = jnp.where(near_lanes, left_down, pltpu.roll(right_down, HALF, 1))

    def terms(e, dp, table, p, halves):
        probs, dscore = [], []
        for i in range(2 * halves):
            rows = slice(HALF * i, HALF * (i + 1))
            first = HEADS * (i % 2)
            prob = e[rows] * table[pl.ds(first + p, 1), :]
            probs.append(prob.astype(BF16))
            dscore.append((prob * (dp[rows] - table[pl.ds(first + PAIRS + p, 1), :])).astype(BF16))
        return jnp.concatenate(probs, axis=0), jnp.concatenate(dscore, axis=0)

    def key_second(p, carry):
        probs, dscore = terms(fa[p], ga[p], za, p, 2)
        dkey = dot(dscore, qa[p])
        dvalue = dot(probs, da[:, :, lanes_of(p)].reshape(GROUP, PAIR))
        more_k, more_v = [], []
        for n in (0, 1):
            probs, dscore = terms(fc[p, n], gc[p, n], zc.at[n], p, 1)
            near_k = dot(dscore, qb[n, p, NEAR])
            near_v = dot(probs, db[n, NEAR, lanes_of(p)])
            probs, dscore = terms(fsd[p, n], gs[p, n], zside.at[n], p, 1)
            more_k.append(near_k + dot(dscore, qb[n, p, SIDE]))
            more_v.append(near_v + dot(probs, db[n, SIDE, lanes_of(p)]))
        dqkv[1, p] = by_heads(dkey + jnp.concatenate(more_k, axis=0))
        dqkv[2, p] = by_heads(dvalue + jnp.concatenate(more_v, axis=0))
        return carry

    each_pair(key_second)

    dvalues = jnp.concatenate([dqkv[2, p].astype(BF16) for p in range(PAIRS)], axis=1)
    total = partial[...] + dot_nt(dvalues, w[:, pl.ds(2 * WIDTH, WIDTH)])
    total = total + dot_nt(through_norm(1), w[:, pl.ds(WIDTH, WIDTH)])
    out_ref[...] = total.astype(BF16)

    for kind in (0, 1):
        for dr in (-1, 1):

            @pl.when(has(dr, 0))
            def _():
                y_copy(kind, dr).wait_send()

        for dc in (-1, 1):

            @pl.when(has(0, dc))
            def _():
                c_copy(kind, dc).wait_send()

            for n in (0, 1):

                @pl.when(jnp.logical_and(halo_from(n), has(0, dc)))
                def _():
                    f_copy(kind, n, dc).wait_send()

    for dr, dc in AROUND:

        @pl.when(has(dr, dc))
        def _():
            z_copy(dr, dc).wait_send()


def per_device(grid_input, w_qkv, out_weight, head_scale, cotangent):
    dma = pltpu.SemaphoreType.DMA
    masked = pltpu.VMEM((PAIRS, 2 * OWN, PAIR), BF16)
    by_pair = pltpu.VMEM((PAIRS, GROUP, PAIR), BF16)
    halo_by_pair = pltpu.VMEM((2, PAIRS, 3 * HALF, PAIR), BF16)
    scores = pltpu.VMEM((PAIRS, 2 * OWN, GROUP), F32)
    near_scores = pltpu.VMEM((PAIRS, 2, OWN, HALF), F32)
    side_scores = pltpu.VMEM((PAIRS, 2, OWN, OWN), F32)
    by_query = pltpu.VMEM((PAIRS, 2 * OWN, OWN), F32)
    hbm = pl.BlockSpec(memory_space=pltpu.HBM)
    result = pl.pallas_call(
        kernel,
        out_shape=jax.ShapeDtypeStruct((OWN, D), BF16),
        in_specs=[hbm] * 5,
        out_specs=pl.BlockSpec(memory_space=pltpu.VMEM),
        scratch_shapes=[
            pltpu.SMEM((HEADS,), F32),
            pltpu.VMEM((3, OWN, D), BF16),
            pltpu.VMEM((3, OWN, D), BF16),
            pltpu.VMEM((3, OWN, WIDTH), BF16),
            pltpu.VMEM((2, 3 * HALF, WIDTH), BF16),
            pltpu.VMEM((D, 3 * WIDTH), BF16),
            pltpu.VMEM((D, WIDTH), BF16),
            pltpu.VMEM((OWN, D), BF16),
            *[by_pair] * 3,
            *[halo_by_pair] * 3,
            *[masked] * 4,
            *[pltpu.VMEM((2, OWN, WIDTH), F32)] * 3,
            pltpu.VMEM((2 * OWN, GROUP), F32),
            pltpu.VMEM((2, OWN, HALF), F32),
            pltpu.VMEM((2, OWN, OWN), F32),
            *[scores] * 4,
            *[near_scores] * 4,
            *[side_scores] * 4,
            *[by_query] * 4,
            pltpu.VMEM((2 * HEADS, OWN), F32),
            pltpu.VMEM((9, 2 * HEADS, OWN), F32),
            pltpu.VMEM((2 * HEADS, GROUP), F32),
            pltpu.VMEM((2, 2 * HEADS, HALF), F32),
            pltpu.VMEM((2, 2 * HEADS, OWN), F32),
            pltpu.VMEM((3, PAIRS, OWN, PAIR), F32),
            pltpu.VMEM((OWN, D), F32),
            dma((5,)),
            dma((4,)),
            dma((4,)),
            dma((4,)),
            dma((4,)),
            dma((8,)),
            dma((8,)),
            dma((9,)),
            dma((9,)),
        ],
        compiler_params=pltpu.CompilerParams(
            collective_id=0, has_side_effects=True, vmem_limit_bytes=60 << 20
        ),
    )(
        head_scale,
        grid_input.reshape(OWN, D),
        w_qkv,
        out_weight,
        cotangent.reshape(OWN, D),
    )
    return result.reshape(TILE_H, TILE_W, D)


def solution(mesh):
    placed = (P("row", "col", None), P(), P(), P(), P("row", "col", None))
    return jax.shard_map(
        per_device, mesh=mesh, in_specs=placed, out_specs=P("row", "col", None), check_vma=False
    )
```

```python
import jax
import jax.numpy as jnp
from jax import lax
from jax.experimental import pallas as pl
from jax.experimental.pallas import tpu as pltpu
from jax.sharding import PartitionSpec as P

D = 1024
HEADS = 8
HEAD_DIM = 64
RADIUS = 8
PAIRS = HEADS // 2
PAIR = 2 * HEAD_DIM
WIDTH = HEADS * HEAD_DIM
TILE_H = 16
TILE_W = 8
OWN = TILE_H * TILE_W
RUN = 8
HALF = OWN // 2
GROUP = 3 * OWN

norm_epsilon = 1e-06

MESH = pl.DeviceIdType.MESH
F32 = jnp.float32
BF16 = jnp.bfloat16
AROUND = [(dr, dc) for dr in (-1, 0, 1) for dc in (-1, 0, 1) if (dr, dc) != (0, 0)]


def slot_of(dr, dc):
    return (dr + 1) * 3 + (dc + 1)


def dot(a, b):
    return lax.dot_general(a, b, (((1,), (0,)), ((), ())), preferred_element_type=F32)


def dot_nt(a, b):
    return lax.dot_general(a, b, (((1,), (1,)), ((), ())), preferred_element_type=F32)


def head_sums(array, ones):
    high = array.astype(BF16)
    low = (array - high.astype(F32)).astype(BF16)
    return dot(high, ones) + dot(low, ones)


def kernel(
    scale_hbm, x_hbm, w_hbm, ow_hbm, cot_hbm, out_ref,
    scale_ref, xa, xb, da, db, w, ow, cot,
    qa, ka, va, qb, kb, vb,
    qm, km, vm, dm, raws, back_own, back_raw,
    mask_a, mask_c, mask_s,
    ea, pa, fa, ga, ec, pc, fc, gc, es, ps, fsd, gs,
    zpart, apart, zbc, dbc, zmine, znear, za, zc, zside,
    dqkv, partial, xrelay, drelay,
    local_sem, ys, yr, cs, cr, fs, fr, zs, zr, rs, rr,
):
    nrow, ncol = lax.axis_size("row"), lax.axis_size("col")
    r, c = lax.axis_index("row"), lax.axis_index("col")

    def has(dr, dc):
        ok = None
        for at, d, n in ((r, dr, nrow), (c, dc, ncol)):
            if d:
                here = at > 0 if d < 0 else at < n - 1
                ok = here if ok is None else jnp.logical_and(ok, here)
        return ok

    def device(dr, dc):
        return (jnp.clip(r + dr, 0, nrow - 1), jnp.clip(c + dc, 0, ncol - 1))

    def remote(src, dst, send, recv, dr, dc):
        return pltpu.make_async_remote_copy(
            src_ref=src, dst_ref=dst, send_sem=send, recv_sem=recv,
            device_id=device(dr, dc), device_id_type=MESH,
        )

    place = lax.rem(c, RUN)
    crosses = {
        1: jnp.logical_and(place == RUN - 1, c < ncol - 1),
        -1: jnp.logical_and(place == 0, c > 0),
    }
    relays = {
        1: jnp.logical_and(place == 1, c < ncol - RUN),
        -1: jnp.logical_and(place == RUN - 2, c >= RUN),
    }
    TO_RELAY, FROM_RELAY = -(RUN - 2), RUN - 1

    barrier = pltpu.get_barrier_semaphore()
    count = 0
    for dr, dc in AROUND:
        there = has(dr, dc)
        count = count + there.astype(jnp.int32)

        @pl.when(there)
        def _():
            pl.semaphore_signal(barrier, inc=1, device_id=device(dr, dc), device_id_type=MESH)

    for dc in (-1, 1):
        count = count + crosses[dc].astype(jnp.int32) + relays[dc].astype(jnp.int32)
        for here, to in ((relays[dc], -TO_RELAY * dc), (crosses[-dc], -FROM_RELAY * dc)):

            @pl.when(here)
            def _():
                pl.semaphore_signal(barrier, inc=1, device_id=device(0, to), device_id_type=MESH)

    local = [
        pltpu.make_async_copy(src, dst, local_sem.at[i])
        for i, (src, dst) in enumerate(
            ((cot_hbm, cot), (ow_hbm, ow), (x_hbm, xa.at[0]), (w_hbm, w), (scale_hbm, scale_ref))
        )
    ]
    for copy in local:
        copy.start()

    def block_of(dc):
        return 0 if dc == 0 else (1 if dc < 0 else 2)

    def half(n):
        return pl.ds(HALF * n, HALF)

    def y_copy(kind, dr):
        mine = 0 if dr < 0 else 1
        src, dst = (x_hbm, xb.at[0, half(1 - mine)]) if kind == 0 else (da.at[0], db.at[1 - mine, half(0)])
        i = 2 * kind + (dr > 0)
        return remote(src.at[half(mine)], dst, ys.at[i], yr.at[i], dr, 0)

    def c_copy(kind, dc):
        src, dst = (x_hbm, xa) if kind == 0 else (da.at[0], da)
        i = 2 * kind + (dc > 0)
        return remote(src, dst.at[block_of(-dc)], cs.at[i], cr.at[i], 0, dc)

    def to_relay(kind, dc):
        src, dst = (x_hbm, xrelay) if kind == 0 else (da.at[0], drelay)
        return remote(src, dst, cs.at[2 * kind + (dc > 0)], rr.at[kind], 0, TO_RELAY * dc)

    def from_relay(kind, dc):
        src, dst = (xrelay, xa) if kind == 0 else (drelay, da)
        i = 2 * kind + (dc > 0)
        return remote(src, dst.at[block_of(-dc)], rs.at[kind], cr.at[i], 0, FROM_RELAY * dc)

    def send_own(kind):
        for dc in (-1, 1):

            @pl.when(jnp.logical_and(has(0, dc), jnp.logical_not(crosses[dc])))
            def _():
                c_copy(kind, dc).start()

            @pl.when(crosses[dc])
            def _():
                to_relay(kind, dc).start()

    def relay(kind):
        for dc in (-1, 1):

            @pl.when(relays[dc])
            def _():
                to_relay(kind, dc).wait_recv()
                from_relay(kind, dc).start()

    def f_copy(kind, n, dc):
        i = 4 * kind + 2 * n + (dc > 0)
        b = block_of(-dc)
        if kind == 0:
            src, dst = xb.at[0, half(n)], xb.at[b, half(n)]
        else:
            src, dst = db.at[n, half(0)], db.at[n, half(b)]
        return remote(src, dst, fs.at[i], fr.at[i], 0, dc)

    def z_copy(dr, dc):
        i = slot_of(dr, dc)
        return remote(zmine, znear.at[slot_of(-dr, -dc)], zs.at[i], zr.at[i], dr, dc)

    def halo_from(n):
        return has(-1, 0) if n == 0 else has(1, 0)

    pl.semaphore_wait(barrier, count)
    for dr in (-1, 1):

        @pl.when(has(dr, 0))
        def _():
            y_copy(0, dr).start()

    send_own(0)

    for dc in (-1, 1):

        @pl.when(jnp.logical_not(has(0, dc)))
        def _():
            b = block_of(dc)
            xa[b] = jnp.zeros((OWN, D), BF16)
            da[b] = jnp.zeros((OWN, WIDTH), BF16)
            xb[b] = jnp.zeros((OWN, D), BF16)
            for n in (0, 1):
                db[n, half(b)] = jnp.zeros((HALF, WIDTH), BF16)

    for n in (0, 1):

        @pl.when(jnp.logical_not(halo_from(n)))
        def _():
            for b in range(3):
                xb[b, half(n)] = jnp.zeros((HALF, D), BF16)
            db[n] = jnp.zeros((3 * HALF, WIDTH), BF16)

    for dr, dc in AROUND:

        @pl.when(jnp.logical_not(has(dr, dc)))
        def _():
            znear[slot_of(dr, dc)] = jnp.zeros((2 * HEADS, OWN), F32)

    local[0].wait()
    local[1].wait()
    for n in range(2):
        cols = pl.ds(256 * n, 256)
        da[0, :, cols] = dot(cot[...], ow[:, cols]).astype(BF16)
    for dr in (-1, 1):

        @pl.when(has(dr, 0))
        def _():
            y_copy(1, dr).start()

    send_own(1)

    local[4].wait()
    local[2].wait()
    local[3].wait()

    def head_ones(n):
        a = lax.broadcasted_iota(jnp.int32, (n, n), 0) // HEAD_DIM
        b = lax.broadcasted_iota(jnp.int32, (n, n), 1) // HEAD_DIM
        return jnp.where(a == b, 1.0, 0.0).astype(BF16)

    def scale_row(first, heads):
        lane = lax.broadcasted_iota(jnp.int32, (1, heads * HEAD_DIM), 1) // HEAD_DIM
        row = jnp.zeros((1, heads * HEAD_DIM), F32)
        for h in range(heads):
            row = jnp.where(lane == h, scale_ref[first + h], row)
        return jnp.sqrt(row)

    quad_rows = [scale_row(0, 4), scale_row(4, 4)]
    ones256 = head_ones(256)

    def window(rows, first_half, lanes, block, halo, first_block):
        row = lax.broadcasted_iota(jnp.int32, (rows, lanes), 0)
        lane = lax.broadcasted_iota(jnp.int32, (rows, lanes), 1)
        own_i = (row // OWN + first_half) * RADIUS + (row % HALF) // TILE_W
        own_j = row % TILE_W
        b = lane // block + first_block
        there_i = (lane % block) // TILE_W
        if halo:
            there_i = there_i - RADIUS if first_half == 0 else there_i + TILE_H
        there_j = lane % TILE_W + jnp.where(b == 0, 0, jnp.where(b == 1, -TILE_W, TILE_W))
        row_at, col_at = r * TILE_H + there_i, c * TILE_W + there_j
        near = (jnp.abs(there_i - own_i) <= RADIUS) & (jnp.abs(there_j - own_j) <= RADIUS)
        inside = (row_at >= 0) & (row_at < nrow * TILE_H) & (col_at >= 0) & (col_at < ncol * TILE_W)
        return jnp.where(near & inside, 1.0, 0.0)

    mask_a[...] = window(2 * OWN, 0, GROUP, OWN, False, 0)
    for n in (0, 1):
        mask_c[n] = window(OWN, n, HALF, HALF, True, 0)
        mask_s[n] = window(OWN, n, OWN, HALF, True, 1)

    relay(0)

    def project(x_rows, store, own=False, chunks=range(6)):
        for n in chunks:
            values = dot(x_rows, w[:, pl.ds(256 * n, 256)])
            kind, quad = n // 2, n % 2
            if kind < 2:
                if own:
                    squares = head_sums(values * values, ones256) + norm_epsilon
                    factor = quad_rows[quad] * lax.rsqrt(squares)
                    cols = pl.ds(256 * quad, 256)
                    raws[kind, :, cols] = values
                    back_own[kind, :, cols] = factor
                    back_raw[kind, :, cols] = factor * values / squares
                else:
                    squares = dot((values * values).astype(BF16), ones256) + norm_epsilon
                    factor = quad_rows[quad] * lax.rsqrt(squares)
                values = values * factor
            result = values.astype(BF16)
            store(kind, 2 * quad, result[:, :PAIR])
            store(kind, 2 * quad + 1, result[:, PAIR:])

    def store_a(first):
        def store(kind, p, result):
            (qa, ka, va)[kind][p, pl.ds(first, result.shape[0])] = result

        return store

    def store_b(first):
        def store(kind, p, result):
            to = (qb, kb, vb)[kind]
            for i in range(result.shape[0] // HALF):
                to[i % 2, p, half(first + i // 2)] = result[HALF * i : HALF * (i + 1)]

        return store

    project(xa[0], store_a(0), own=True)
    first_lanes = lax.broadcasted_iota(jnp.int32, (HALF, PAIR), 1) < HEAD_DIM
    zero = jnp.zeros((HALF, PAIR), BF16)
    for p in range(PAIRS):
        for to, values in (
            (qm, qa[p, pl.ds(0, OWN)]), (km, ka[p, pl.ds(0, OWN)]), (vm, va[p, pl.ds(0, OWN)]),
            (dm, da[0, :, pl.ds(PAIR * p, PAIR)]),
        ):
            for n in (0, 1):
                rows = values[HALF * n : HALF * (n + 1)]
                to[p, half(2 * n)] = jnp.where(first_lanes, rows, zero)
                to[p, half(2 * n + 1)] = jnp.where(first_lanes, zero, rows)

    def pass_on(kind):
        for n, dr in ((0, 1), (1, -1)):

            @pl.when(halo_from(n))
            def _():
                y_copy(kind, dr).wait_recv()
                for dc in (-1, 1):

                    @pl.when(has(0, dc))
                    def _():
                        f_copy(kind, n, dc).start()

    def corners(kind):
        for n in (0, 1):
            for dc in (-1, 1):

                @pl.when(jnp.logical_and(halo_from(n), has(0, -dc)))
                def _():
                    f_copy(kind, n, dc).wait_recv()

    def lanes_of(p):
        return pl.ds(pl.multiple_of(p * PAIR, PAIR), PAIR)

    NEAR, SIDE = pl.ds(0, HALF), pl.ds(HALF, OWN)

    def rows_of(n):
        return pl.ds(OWN * n, OWN)

    def each_pair(body):
        lax.fori_loop(0, PAIRS, body, 0, unroll=True)

    pass_on(0)
    project(xb[0], store_b(0))

    def near_scores(p, carry):
        z, along = [], []
        for n in (0, 1):
            e = jnp.exp(dot_nt(qm[p, rows_of(n)], kb[n, p, NEAR])) * mask_c[n]
            dp = dot_nt(dm[p, rows_of(n)], vb[n, p, NEAR])
            ec[p, n] = e
            pc[p, n] = dp
            fc[p, n] = jnp.exp(dot_nt(km[p, rows_of(n)], qb[n, p, NEAR])) * mask_c[n]
            z.append(e)
            along.append(e * dp)
        rest = jnp.zeros((2 * OWN, HALF), F32)
        zpart[p] = jnp.concatenate([jnp.concatenate(z, axis=0), rest], axis=1)
        apart[p] = jnp.concatenate([jnp.concatenate(along, axis=0), rest], axis=1)
        return carry

    each_pair(near_scores)

    relay(1)
    for dc in (-1, 1):

        @pl.when(has(0, -dc))
        def _():
            c_copy(0, dc).wait_recv()

    project(xa[1:3].reshape(2 * OWN, D), store_a(OWN))

    def tiles(array):
        return array[:, :OWN] + array[:, OWN : 2 * OWN] + array[:, 2 * OWN :]

    def query_a(p, carry):
        e = jnp.exp(dot_nt(qm[p], ka[p])) * mask_a[...]
        dp = dot_nt(dm[p], va[p])
        ea[p] = e
        pa[p] = dp
        zpart[p] = zpart[p] + tiles(e)
        apart[p] = apart[p] + tiles(e * dp)
        return carry

    lax.fori_loop(0, PAIRS, query_a, 0, unroll=True)

    pass_on(1)
    corners(0)
    x_sides = xb[1:3].reshape(2 * OWN, D)
    project(x_sides, store_b(1), chunks=range(2, 6))

    lane = lax.broadcasted_iota(jnp.int32, (2 * OWN, OWN), 1)

    def side_scores(p, table):
        z, along = [], []
        for n in (0, 1):
            e = jnp.exp(dot_nt(qm[p, rows_of(n)], kb[n, p, SIDE])) * mask_s[n]
            dp = dot_nt(dm[p, rows_of(n)], vb[n, p, SIDE])
            es[p, n] = e
            ps[p, n] = dp
            z.append(e)
            along.append(e * dp)
        z = jnp.sum(jnp.concatenate(z, axis=0) + zpart[p], axis=1, keepdims=True)
        along = jnp.sum(jnp.concatenate(along, axis=0) + apart[p], axis=1, keepdims=True)
        inverse = 1.0 / z
        delta = along * inverse
        zbc[p] = jnp.broadcast_to(inverse, (2 * OWN, OWN))
        dbc[p] = jnp.broadcast_to(delta, (2 * OWN, OWN))
        table = jnp.where(lane == p, inverse, table)
        return jnp.where(lane == PAIRS + p, delta, table)

    table = lax.fori_loop(0, PAIRS, side_scores, jnp.zeros((2 * OWN, OWN), F32), unroll=True)
    upper, lower = table[:OWN].T[:HEADS], table[OWN:].T[:HEADS]
    left_lanes = lax.broadcasted_iota(jnp.int32, (HEADS, OWN), 1) < HALF
    zmine[pl.ds(0, HEADS)] = jnp.where(left_lanes, upper, pltpu.roll(lower, HALF, 1))
    zmine[pl.ds(HEADS, HEADS)] = jnp.where(left_lanes, pltpu.roll(upper, HALF, 1), lower)
    for dr, dc in AROUND:

        @pl.when(has(dr, dc))
        def _():
            z_copy(dr, dc).start()


    project(x_sides, store_b(1), chunks=range(2))

    def key_sides(p, carry):
        for n in (0, 1):
            fsd[p, n] = jnp.exp(dot_nt(km[p, rows_of(n)], qb[n, p, SIDE])) * mask_s[n]
        return carry

    each_pair(key_sides)

    for dc in (-1, 1):

        @pl.when(has(0, -dc))
        def _():
            c_copy(1, dc).wait_recv()

    def key_a(p, carry):
        fa[p] = jnp.exp(dot_nt(km[p], qa[p])) * mask_a[...]
        ga[p] = dot_nt(vm[p], da[:, :, lanes_of(p)].reshape(GROUP, PAIR))
        return carry

    each_pair(key_a)

    def by_heads(array):
        parts = [array[HALF * i : HALF * (i + 1)] for i in range(4)]
        return jnp.concatenate(
            [jnp.where(first_lanes, parts[2 * n], parts[2 * n + 1]) for n in (0, 1)], axis=0
        )

    def query_second(p, carry):
        inverse, delta = zbc[p], dbc[p]
        wide = jnp.concatenate([inverse] * 3, axis=1)
        dscore = ea[p] * wide * (pa[p] - jnp.concatenate([delta] * 3, axis=1))
        result = dot(dscore.astype(BF16), ka[p])
        more = []
        for n in (0, 1):
            rows = slice(OWN * n, OWN * (n + 1))
            dscore = ec[p, n] * inverse[rows, :HALF] * (pc[p, n] - delta[rows, :HALF])
            near = dot(dscore.astype(BF16), kb[n, p, NEAR])
            dscore = es[p, n] * inverse[rows] * (ps[p, n] - delta[rows])
            more.append(near + dot(dscore.astype(BF16), kb[n, p, SIDE]))
        dqkv[0, p] = by_heads(result + jnp.concatenate(more, axis=0))
        return carry

    each_pair(query_second)
    ones128 = head_ones(PAIR)

    def through_norm(kind):
        blocks = []
        for p in range(PAIRS):
            grads = dqkv[kind, p]
            cols = pl.ds(PAIR * p, PAIR)
            along = head_sums(grads * raws[kind, :, cols], ones128)
            blocks.append(
                (back_own[kind, :, cols] * grads - back_raw[kind, :, cols] * along).astype(BF16)
            )
        return jnp.concatenate(blocks, axis=1)

    partial[...] = dot_nt(through_norm(0), w[:, pl.ds(0, WIDTH)])

    corners(1)

    def key_halo_cot(p, carry):
        for n in (0, 1):
            gc[p, n] = dot_nt(vm[p, rows_of(n)], db[n, NEAR, lanes_of(p)])
            gs[p, n] = dot_nt(vm[p, rows_of(n)], db[n, SIDE, lanes_of(p)])
        return carry

    each_pair(key_halo_cot)

    for dr, dc in AROUND:

        @pl.when(has(dr, dc))
        def _():
            z_copy(-dr, -dc).wait_recv()

    znear[slot_of(0, 0)] = zmine[...]
    near_lanes = lax.broadcasted_iota(jnp.int32, (2 * HEADS, OWN), 1) < HALF
    for b, dc in enumerate((0, -1, 1)):
        za[:, pl.ds(b * OWN, OWN)] = znear[slot_of(0, dc)]
    own_up, left_up, right_up = (znear[slot_of(-1, dc)] for dc in (0, -1, 1))
    zc[0] = pltpu.roll(own_up, HALF, 1)[:, :HALF]
    zside[0] = jnp.where(near_lanes, pltpu.roll(left_up, HALF, 1), right_up)
    own_down, left_down, right_down = (znear[slot_of(1, dc)] for dc in (0, -1, 1))
    zc[1] = own_down[:, :HALF]
    zside[1] = jnp.where(near_lanes, left_down, pltpu.roll(right_down, HALF, 1))

    def terms(e, dp, table, p, halves):
        probs, dscore = [], []
        for i in range(2 * halves):
            rows = slice(HALF * i, HALF * (i + 1))
            first = HEADS * (i % 2)
            prob = e[rows] * table[pl.ds(first + p, 1), :]
            probs.append(prob.astype(BF16))
            dscore.append((prob * (dp[rows] - table[pl.ds(first + PAIRS + p, 1), :])).astype(BF16))
        return jnp.concatenate(probs, axis=0), jnp.concatenate(dscore, axis=0)

    def key_second(p, carry):
        probs, dscore = terms(fa[p], ga[p], za, p, 2)
        dkey = dot(dscore, qa[p])
        dvalue = dot(probs, da[:, :, lanes_of(p)].reshape(GROUP, PAIR))
        more_k, more_v = [], []
        for n in (0, 1):
            probs, dscore = terms(fc[p, n], gc[p, n], zc.at[n], p, 1)
            near_k = dot(dscore, qb[n, p, NEAR])
            near_v = dot(probs, db[n, NEAR, lanes_of(p)])
            probs, dscore = terms(fsd[p, n], gs[p, n], zside.at[n], p, 1)
            more_k.append(near_k + dot(dscore, qb[n, p, SIDE]))
            more_v.append(near_v + dot(probs, db[n, SIDE, lanes_of(p)]))
        dqkv[1, p] = by_heads(dkey + jnp.concatenate(more_k, axis=0))
        dqkv[2, p] = by_heads(dvalue + jnp.concatenate(more_v, axis=0))
        return carry

    each_pair(key_second)

    dvalues = jnp.concatenate([dqkv[2, p].astype(BF16) for p in range(PAIRS)], axis=1)
    total = partial[...] + dot_nt(dvalues, w[:, pl.ds(2 * WIDTH, WIDTH)])
    total = total + dot_nt(through_norm(1), w[:, pl.ds(WIDTH, WIDTH)])
    out_ref[...] = total.astype(BF16)

    for kind in (0, 1):
        for dr in (-1, 1):

            @pl.when(has(dr, 0))
            def _():
                y_copy(kind, dr).wait_send()

        for dc in (-1, 1):

            @pl.when(has(0, dc))
            def _():
                c_copy(kind, dc).wait_send()

            @pl.when(relays[dc])
            def _():
                from_relay(kind, dc).wait_send()

            for n in (0, 1):

                @pl.when(jnp.logical_and(halo_from(n), has(0, dc)))
                def _():
                    f_copy(kind, n, dc).wait_send()

    for dr, dc in AROUND:

        @pl.when(has(dr, dc))
        def _():
            z_copy(dr, dc).wait_send()


def per_device(grid_input, w_qkv, out_weight, head_scale, cotangent):
    dma = pltpu.SemaphoreType.DMA
    masked = pltpu.VMEM((PAIRS, 2 * OWN, PAIR), BF16)
    by_pair = pltpu.VMEM((PAIRS, GROUP, PAIR), BF16)
    halo_by_pair = pltpu.VMEM((2, PAIRS, 3 * HALF, PAIR), BF16)
    scores = pltpu.VMEM((PAIRS, 2 * OWN, GROUP), F32)
    near_scores = pltpu.VMEM((PAIRS, 2, OWN, HALF), F32)
    side_scores = pltpu.VMEM((PAIRS, 2, OWN, OWN), F32)
    by_query = pltpu.VMEM((PAIRS, 2 * OWN, OWN), F32)
    hbm = pl.BlockSpec(memory_space=pltpu.HBM)
    result = pl.pallas_call(
        kernel,
        out_shape=jax.ShapeDtypeStruct((OWN, D), BF16),
        in_specs=[hbm] * 5,
        out_specs=pl.BlockSpec(memory_space=pltpu.VMEM),
        scratch_shapes=[
            pltpu.SMEM((HEADS,), F32),
            pltpu.VMEM((3, OWN, D), BF16),
            pltpu.VMEM((3, OWN, D), BF16),
            pltpu.VMEM((3, OWN, WIDTH), BF16),
            pltpu.VMEM((2, 3 * HALF, WIDTH), BF16),
            pltpu.VMEM((D, 3 * WIDTH), BF16),
            pltpu.VMEM((D, WIDTH), BF16),
            pltpu.VMEM((OWN, D), BF16),
            *[by_pair] * 3,
            *[halo_by_pair] * 3,
            *[masked] * 4,
            *[pltpu.VMEM((2, OWN, WIDTH), F32)] * 3,
            pltpu.VMEM((2 * OWN, GROUP), F32),
            pltpu.VMEM((2, OWN, HALF), F32),
            pltpu.VMEM((2, OWN, OWN), F32),
            *[scores] * 4,
            *[near_scores] * 4,
            *[side_scores] * 4,
            *[by_query] * 4,
            pltpu.VMEM((2 * HEADS, OWN), F32),
            pltpu.VMEM((9, 2 * HEADS, OWN), F32),
            pltpu.VMEM((2 * HEADS, GROUP), F32),
            pltpu.VMEM((2, 2 * HEADS, HALF), F32),
            pltpu.VMEM((2, 2 * HEADS, OWN), F32),
            pltpu.VMEM((3, PAIRS, OWN, PAIR), F32),
            pltpu.VMEM((OWN, D), F32),
            pltpu.VMEM((OWN, D), BF16),
            pltpu.VMEM((OWN, WIDTH), BF16),
            dma((5,)),
            dma((4,)),
            dma((4,)),
            dma((4,)),
            dma((4,)),
            dma((8,)),
            dma((8,)),
            dma((9,)),
            dma((9,)),
            dma((2,)),
            dma((2,)),
        ],
        compiler_params=pltpu.CompilerParams(
            collective_id=0, has_side_effects=True, vmem_limit_bytes=60 << 20
        ),
    )(
        head_scale,
        grid_input.reshape(OWN, D),
        w_qkv,
        out_weight,
        cotangent.reshape(OWN, D),
    )
    return result.reshape(TILE_H, TILE_W, D)


def solution(mesh):
    placed = (P("row", "col", None), P(), P(), P(), P("row", "col", None))
    return jax.shard_map(
        per_device, mesh=mesh, in_specs=placed, out_specs=P("row", "col", None), check_vma=False
    )
```

```python
import jax
import jax.numpy as jnp
from jax import lax
from jax.experimental import pallas as pl
from jax.experimental.pallas import tpu as pltpu
from jax.sharding import PartitionSpec as P

D = 1024
HEADS = 8
HEAD_DIM = 64
RADIUS = 8
PAIRS = HEADS // 2
PAIR = 2 * HEAD_DIM
WIDTH = HEADS * HEAD_DIM
TILE_H = 16
TILE_W = 8
OWN = TILE_H * TILE_W
RUN = 8
HALF = OWN // 2
GROUP = 3 * OWN

norm_epsilon = 1e-06

MESH = pl.DeviceIdType.MESH
F32 = jnp.float32
BF16 = jnp.bfloat16
AROUND = [(dr, dc) for dr in (-1, 0, 1) for dc in (-1, 0, 1) if (dr, dc) != (0, 0)]


def slot_of(dr, dc):
    return (dr + 1) * 3 + (dc + 1)


def dot(a, b):
    return lax.dot_general(a, b, (((1,), (0,)), ((), ())), preferred_element_type=F32)


def dot_nt(a, b):
    return lax.dot_general(a, b, (((1,), (1,)), ((), ())), preferred_element_type=F32)


def head_sums(array, ones):
    high = array.astype(BF16)
    low = (array - high.astype(F32)).astype(BF16)
    return dot(high, ones) + dot(low, ones)


def kernel(
    scale_hbm, x_hbm, w_hbm, ow_hbm, cot_hbm, out_ref,
    scale_ref, xa, xb, da, db, w, ow, cot,
    qa, ka, va, qb, kb, vb,
    qm, km, vm, dm, raws, back_own, back_raw,
    mask_a, mask_c, mask_s,
    ea, pa, fa, ga, ec, pc, fc, gc, es, ps, fsd, gs,
    zpart, apart, zbc, dbc, zmine, znear, za, zc, zside,
    dqkv, partial, xrelay, drelay,
    local_sem, ys, yr, cs, cr, fs, fr, zs, zr, rs, rr,
):
    nrow, ncol = lax.axis_size("row"), lax.axis_size("col")
    r, c = lax.axis_index("row"), lax.axis_index("col")

    def has(dr, dc):
        ok = None
        for at, d, n in ((r, dr, nrow), (c, dc, ncol)):
            if d:
                here = at > 0 if d < 0 else at < n - 1
                ok = here if ok is None else jnp.logical_and(ok, here)
        return ok

    def device(dr, dc):
        return (jnp.clip(r + dr, 0, nrow - 1), jnp.clip(c + dc, 0, ncol - 1))

    def remote(src, dst, send, recv, dr, dc):
        return pltpu.make_async_remote_copy(
            src_ref=src, dst_ref=dst, send_sem=send, recv_sem=recv,
            device_id=device(dr, dc), device_id_type=MESH,
        )

    place = lax.rem(c, RUN)
    crosses = {
        1: jnp.logical_and(place == RUN - 1, c < ncol - 1),
        -1: jnp.logical_and(place == 0, c > 0),
    }
    relays = {
        1: jnp.logical_and(place == 1, c < ncol - RUN),
        -1: jnp.logical_and(place == RUN - 2, c >= RUN),
    }
    TO_RELAY, FROM_RELAY = -(RUN - 2), RUN - 1

    barrier = pltpu.get_barrier_semaphore()
    count = 0
    for dr, dc in AROUND:
        there = has(dr, dc)
        count = count + there.astype(jnp.int32)

        @pl.when(there)
        def _():
            pl.semaphore_signal(barrier, inc=1, device_id=device(dr, dc), device_id_type=MESH)

    for dc in (-1, 1):
        count = count + crosses[dc].astype(jnp.int32) + relays[dc].astype(jnp.int32)
        for here, to in ((relays[dc], -TO_RELAY * dc), (crosses[-dc], -FROM_RELAY * dc)):

            @pl.when(here)
            def _():
                pl.semaphore_signal(barrier, inc=1, device_id=device(0, to), device_id_type=MESH)

    local = [
        pltpu.make_async_copy(src, dst, local_sem.at[i])
        for i, (src, dst) in enumerate(
            ((cot_hbm, cot), (ow_hbm, ow), (x_hbm, xa.at[0]), (w_hbm, w), (scale_hbm, scale_ref))
        )
    ]
    for copy in local:
        copy.start()

    def block_of(dc):
        return 0 if dc == 0 else (1 if dc < 0 else 2)

    def half(n):
        return pl.ds(HALF * n, HALF)

    def y_copy(kind, dr):
        mine = 0 if dr < 0 else 1
        src, dst = (x_hbm, xb.at[0, half(1 - mine)]) if kind == 0 else (da.at[0], db.at[1 - mine, half(0)])
        i = 2 * kind + (dr > 0)
        return remote(src.at[half(mine)], dst, ys.at[i], yr.at[i], dr, 0)

    def c_copy(kind, dc):
        src, dst = (x_hbm, xa) if kind == 0 else (da.at[0], da)
        i = 2 * kind + (dc > 0)
        return remote(src, dst.at[block_of(-dc)], cs.at[i], cr.at[i], 0, dc)

    def to_relay(kind, dc):
        src, dst = (x_hbm, xrelay) if kind == 0 else (da.at[0], drelay)
        return remote(src, dst, cs.at[2 * kind + (dc > 0)], rr.at[kind], 0, TO_RELAY * dc)

    def from_relay(kind, dc):
        src, dst = (xrelay, xa) if kind == 0 else (drelay, da)
        i = 2 * kind + (dc > 0)
        return remote(src, dst.at[block_of(-dc)], rs.at[kind], cr.at[i], 0, FROM_RELAY * dc)

    def send_own(kind):
        for dc in (-1, 1):

            @pl.when(jnp.logical_and(has(0, dc), jnp.logical_not(crosses[dc])))
            def _():
                c_copy(kind, dc).start()

            @pl.when(crosses[dc])
            def _():
                to_relay(kind, dc).start()

    def relay(kind):
        for dc in (-1, 1):

            @pl.when(relays[dc])
            def _():
                to_relay(kind, dc).wait_recv()
                from_relay(kind, dc).start()

    def f_copy(kind, n, dc):
        i = 4 * kind + 2 * n + (dc > 0)
        b = block_of(-dc)
        if kind == 0:
            src, dst = xb.at[0, half(n)], xb.at[b, half(n)]
        else:
            src, dst = db.at[n, half(0)], db.at[n, half(b)]
        return remote(src, dst, fs.at[i], fr.at[i], 0, dc)

    def z_copy(dr, dc):
        i = slot_of(dr, dc)
        return remote(zmine, znear.at[slot_of(-dr, -dc)], zs.at[i], zr.at[i], dr, dc)

    def halo_from(n):
        return has(-1, 0) if n == 0 else has(1, 0)

    pl.semaphore_wait(barrier, count)
    for dr in (-1, 1):

        @pl.when(has(dr, 0))
        def _():
            y_copy(0, dr).start()

    send_own(0)

    for dc in (-1, 1):

        @pl.when(jnp.logical_not(has(0, dc)))
        def _():
            b = block_of(dc)
            xa[b] = jnp.zeros((OWN, D), BF16)
            da[b] = jnp.zeros((OWN, WIDTH), BF16)
            xb[b] = jnp.zeros((OWN, D), BF16)
            for n in (0, 1):
                db[n, half(b)] = jnp.zeros((HALF, WIDTH), BF16)

    for n in (0, 1):

        @pl.when(jnp.logical_not(halo_from(n)))
        def _():
            for b in range(3):
                xb[b, half(n)] = jnp.zeros((HALF, D), BF16)
            db[n] = jnp.zeros((3 * HALF, WIDTH), BF16)

    for dr, dc in AROUND:

        @pl.when(jnp.logical_not(has(dr, dc)))
        def _():
            znear[slot_of(dr, dc)] = jnp.zeros((2 * HEADS, OWN), F32)

    local[0].wait()
    local[1].wait()
    for n in range(2):
        cols = pl.ds(256 * n, 256)
        da[0, :, cols] = dot(cot[...], ow[:, cols]).astype(BF16)
    send_own(1)

    local[4].wait()
    local[2].wait()
    local[3].wait()

    def head_ones(n):
        a = lax.broadcasted_iota(jnp.int32, (n, n), 0) // HEAD_DIM
        b = lax.broadcasted_iota(jnp.int32, (n, n), 1) // HEAD_DIM
        return jnp.where(a == b, 1.0, 0.0).astype(BF16)

    def scale_row(first, heads):
        lane = lax.broadcasted_iota(jnp.int32, (1, heads * HEAD_DIM), 1) // HEAD_DIM
        row = jnp.zeros((1, heads * HEAD_DIM), F32)
        for h in range(heads):
            row = jnp.where(lane == h, scale_ref[first + h], row)
        return jnp.sqrt(row)

    quad_rows = [scale_row(0, 4), scale_row(4, 4)]
    ones256 = head_ones(256)

    def window(rows, first_half, lanes, block, halo, first_block):
        row = lax.broadcasted_iota(jnp.int32, (rows, lanes), 0)
        lane = lax.broadcasted_iota(jnp.int32, (rows, lanes), 1)
        own_i = (row // OWN + first_half) * RADIUS + (row % HALF) // TILE_W
        own_j = row % TILE_W
        b = lane // block + first_block
        there_i = (lane % block) // TILE_W
        if halo:
            there_i = there_i - RADIUS if first_half == 0 else there_i + TILE_H
        there_j = lane % TILE_W + jnp.where(b == 0, 0, jnp.where(b == 1, -TILE_W, TILE_W))
        row_at, col_at = r * TILE_H + there_i, c * TILE_W + there_j
        near = (jnp.abs(there_i - own_i) <= RADIUS) & (jnp.abs(there_j - own_j) <= RADIUS)
        inside = (row_at >= 0) & (row_at < nrow * TILE_H) & (col_at >= 0) & (col_at < ncol * TILE_W)
        return jnp.where(near & inside, 1.0, 0.0)

    mask_a[...] = window(2 * OWN, 0, GROUP, OWN, False, 0)
    for n in (0, 1):
        mask_c[n] = window(OWN, n, HALF, HALF, True, 0)
        mask_s[n] = window(OWN, n, OWN, HALF, True, 1)

    relay(0)

    def project(x_rows, store, own=False, chunks=range(6)):
        for n in chunks:
            values = dot(x_rows, w[:, pl.ds(256 * n, 256)])
            kind, quad = n // 2, n % 2
            if kind < 2:
                if own:
                    squares = head_sums(values * values, ones256) + norm_epsilon
                    factor = quad_rows[quad] * lax.rsqrt(squares)
                    cols = pl.ds(256 * quad, 256)
                    raws[kind, :, cols] = values
                    back_own[kind, :, cols] = factor
                    back_raw[kind, :, cols] = factor * values / squares
                else:
                    squares = head_sums(values * values, ones256) + norm_epsilon
                    factor = quad_rows[quad] * lax.rsqrt(squares)
                values = values * factor
            result = values.astype(BF16)
            store(kind, 2 * quad, result[:, :PAIR])
            store(kind, 2 * quad + 1, result[:, PAIR:])

    def store_a(first):
        def store(kind, p, result):
            (qa, ka, va)[kind][p, pl.ds(first, result.shape[0])] = result

        return store

    def store_b(first):
        def store(kind, p, result):
            to = (qb, kb, vb)[kind]
            for i in range(result.shape[0] // HALF):
                to[i % 2, p, half(first + i // 2)] = result[HALF * i : HALF * (i + 1)]

        return store

    project(xa[0], store_a(0), own=True)
    for dr in (-1, 1):

        @pl.when(has(dr, 0))
        def _():
            y_copy(1, dr).start()

    first_lanes = lax.broadcasted_iota(jnp.int32, (HALF, PAIR), 1) < HEAD_DIM
    zero = jnp.zeros((HALF, PAIR), BF16)
    for p in range(PAIRS):
        for to, values in (
            (qm, qa[p, pl.ds(0, OWN)]), (km, ka[p, pl.ds(0, OWN)]), (vm, va[p, pl.ds(0, OWN)]),
            (dm, da[0, :, pl.ds(PAIR * p, PAIR)]),
        ):
            for n in (0, 1):
                rows = values[HALF * n : HALF * (n + 1)]
                to[p, half(2 * n)] = jnp.where(first_lanes, rows, zero)
                to[p, half(2 * n + 1)] = jnp.where(first_lanes, zero, rows)

    def pass_on(kind):
        for n, dr in ((0, 1), (1, -1)):

            @pl.when(halo_from(n))
            def _():
                y_copy(kind, dr).wait_recv()
                for dc in (-1, 1):

                    @pl.when(has(0, dc))
                    def _():
                        f_copy(kind, n, dc).start()

    def corners(kind):
        for n in (0, 1):
            for dc in (-1, 1):

                @pl.when(jnp.logical_and(halo_from(n), has(0, -dc)))
                def _():
                    f_copy(kind, n, dc).wait_recv()

    def lanes_of(p):
        return pl.ds(pl.multiple_of(p * PAIR, PAIR), PAIR)

    NEAR, SIDE = pl.ds(0, HALF), pl.ds(HALF, OWN)

    def rows_of(n):
        return pl.ds(OWN * n, OWN)

    def each_pair(body):
        lax.fori_loop(0, PAIRS, body, 0, unroll=True)

    pass_on(0)
    project(xb[0], store_b(0))

    def near_scores(p, carry):
        z, along = [], []
        for n in (0, 1):
            e = jnp.exp(dot_nt(qm[p, rows_of(n)], kb[n, p, NEAR])) * mask_c[n]
            dp = dot_nt(dm[p, rows_of(n)], vb[n, p, NEAR])
            ec[p, n] = e
            pc[p, n] = dp
            fc[p, n] = jnp.exp(dot_nt(km[p, rows_of(n)], qb[n, p, NEAR])) * mask_c[n]
            z.append(e)
            along.append(e * dp)
        rest = jnp.zeros((2 * OWN, HALF), F32)
        zpart[p] = jnp.concatenate([jnp.concatenate(z, axis=0), rest], axis=1)
        apart[p] = jnp.concatenate([jnp.concatenate(along, axis=0), rest], axis=1)
        return carry

    each_pair(near_scores)

    relay(1)
    for dc in (-1, 1):

        @pl.when(has(0, -dc))
        def _():
            c_copy(0, dc).wait_recv()

    project(xa[1:3].reshape(2 * OWN, D), store_a(OWN))

    def tiles(array):
        return array[:, :OWN] + array[:, OWN : 2 * OWN] + array[:, 2 * OWN :]

    def query_a(p, carry):
        e = jnp.exp(dot_nt(qm[p], ka[p])) * mask_a[...]
        dp = dot_nt(dm[p], va[p])
        ea[p] = e
        pa[p] = dp
        zpart[p] = zpart[p] + tiles(e)
        apart[p] = apart[p] + tiles(e * dp)
        return carry

    lax.fori_loop(0, PAIRS, query_a, 0, unroll=True)

    corners(0)
    x_sides = xb[1:3].reshape(2 * OWN, D)
    project(x_sides, store_b(1), chunks=range(2, 6))

    lane = lax.broadcasted_iota(jnp.int32, (2 * OWN, OWN), 1)

    def side_scores(p, table):
        z, along = [], []
        for n in (0, 1):
            e = jnp.exp(dot_nt(qm[p, rows_of(n)], kb[n, p, SIDE])) * mask_s[n]
            dp = dot_nt(dm[p, rows_of(n)], vb[n, p, SIDE])
            es[p, n] = e
            ps[p, n] = dp
            z.append(e)
            along.append(e * dp)
        z = jnp.sum(jnp.concatenate(z, axis=0) + zpart[p], axis=1, keepdims=True)
        along = jnp.sum(jnp.concatenate(along, axis=0) + apart[p], axis=1, keepdims=True)
        inverse = 1.0 / z
        delta = along * inverse
        zbc[p] = jnp.broadcast_to(inverse, (2 * OWN, OWN))
        dbc[p] = jnp.broadcast_to(delta, (2 * OWN, OWN))
        table = jnp.where(lane == p, inverse, table)
        return jnp.where(lane == PAIRS + p, delta, table)

    table = lax.fori_loop(0, PAIRS, side_scores, jnp.zeros((2 * OWN, OWN), F32), unroll=True)
    upper, lower = table[:OWN].T[:HEADS], table[OWN:].T[:HEADS]
    left_lanes = lax.broadcasted_iota(jnp.int32, (HEADS, OWN), 1) < HALF
    zmine[pl.ds(0, HEADS)] = jnp.where(left_lanes, upper, pltpu.roll(lower, HALF, 1))
    zmine[pl.ds(HEADS, HEADS)] = jnp.where(left_lanes, pltpu.roll(upper, HALF, 1), lower)
    for dr, dc in AROUND:

        @pl.when(has(dr, dc))
        def _():
            z_copy(dr, dc).start()

    pass_on(1)

    project(x_sides, store_b(1), chunks=range(2))

    def key_sides(p, carry):
        for n in (0, 1):
            fsd[p, n] = jnp.exp(dot_nt(km[p, rows_of(n)], qb[n, p, SIDE])) * mask_s[n]
        return carry

    each_pair(key_sides)

    for dc in (-1, 1):

        @pl.when(has(0, -dc))
        def _():
            c_copy(1, dc).wait_recv()

    def key_a(p, carry):
        fa[p] = jnp.exp(dot_nt(km[p], qa[p])) * mask_a[...]
        ga[p] = dot_nt(vm[p], da[:, :, lanes_of(p)].reshape(GROUP, PAIR))
        return carry

    each_pair(key_a)

    def by_heads(array):
        parts = [array[HALF * i : HALF * (i + 1)] for i in range(4)]
        return jnp.concatenate(
            [jnp.where(first_lanes, parts[2 * n], parts[2 * n + 1]) for n in (0, 1)], axis=0
        )

    def query_second(p, carry):
        inverse, delta = zbc[p], dbc[p]
        wide = jnp.concatenate([inverse] * 3, axis=1)
        dscore = ea[p] * wide * (pa[p] - jnp.concatenate([delta] * 3, axis=1))
        result = dot(dscore.astype(BF16), ka[p])
        more = []
        for n in (0, 1):
            rows = slice(OWN * n, OWN * (n + 1))
            dscore = ec[p, n] * inverse[rows, :HALF] * (pc[p, n] - delta[rows, :HALF])
            near = dot(dscore.astype(BF16), kb[n, p, NEAR])
            dscore = es[p, n] * inverse[rows] * (ps[p, n] - delta[rows])
            more.append(near + dot(dscore.astype(BF16), kb[n, p, SIDE]))
        dqkv[0, p] = by_heads(result + jnp.concatenate(more, axis=0))
        return carry

    each_pair(query_second)
    ones128 = head_ones(PAIR)

    def through_norm(kind):
        blocks = []
        for p in range(PAIRS):
            grads = dqkv[kind, p]
            cols = pl.ds(PAIR * p, PAIR)
            along = head_sums(grads * raws[kind, :, cols], ones128)
            blocks.append(
                (back_own[kind, :, cols] * grads - back_raw[kind, :, cols] * along).astype(BF16)
            )
        return jnp.concatenate(blocks, axis=1)

    partial[...] = dot_nt(through_norm(0), w[:, pl.ds(0, WIDTH)])

    corners(1)

    def key_halo_cot(p, carry):
        for n in (0, 1):
            gc[p, n] = dot_nt(vm[p, rows_of(n)], db[n, NEAR, lanes_of(p)])
            gs[p, n] = dot_nt(vm[p, rows_of(n)], db[n, SIDE, lanes_of(p)])
        return carry

    each_pair(key_halo_cot)

    for dr, dc in AROUND:

        @pl.when(has(dr, dc))
        def _():
            z_copy(-dr, -dc).wait_recv()

    znear[slot_of(0, 0)] = zmine[...]
    near_lanes = lax.broadcasted_iota(jnp.int32, (2 * HEADS, OWN), 1) < HALF
    for b, dc in enumerate((0, -1, 1)):
        za[:, pl.ds(b * OWN, OWN)] = znear[slot_of(0, dc)]
    own_up, left_up, right_up = (znear[slot_of(-1, dc)] for dc in (0, -1, 1))
    zc[0] = pltpu.roll(own_up, HALF, 1)[:, :HALF]
    zside[0] = jnp.where(near_lanes, pltpu.roll(left_up, HALF, 1), right_up)
    own_down, left_down, right_down = (znear[slot_of(1, dc)] for dc in (0, -1, 1))
    zc[1] = own_down[:, :HALF]
    zside[1] = jnp.where(near_lanes, left_down, pltpu.roll(right_down, HALF, 1))

    def terms(e, dp, table, p, halves):
        probs, dscore = [], []
        for i in range(2 * halves):
            rows = slice(HALF * i, HALF * (i + 1))
            first = HEADS * (i % 2)
            prob = e[rows] * table[pl.ds(first + p, 1), :]
            probs.append(prob.astype(BF16))
            dscore.append((prob * (dp[rows] - table[pl.ds(first + PAIRS + p, 1), :])).astype(BF16))
        return jnp.concatenate(probs, axis=0), jnp.concatenate(dscore, axis=0)

    def key_second(p, carry):
        probs, dscore = terms(fa[p], ga[p], za, p, 2)
        dkey = dot(dscore, qa[p])
        dvalue = dot(probs, da[:, :, lanes_of(p)].reshape(GROUP, PAIR))
        more_k, more_v = [], []
        for n in (0, 1):
            probs, dscore = terms(fc[p, n], gc[p, n], zc.at[n], p, 1)
            near_k = dot(dscore, qb[n, p, NEAR])
            near_v = dot(probs, db[n, NEAR, lanes_of(p)])
            probs, dscore = terms(fsd[p, n], gs[p, n], zside.at[n], p, 1)
            more_k.append(near_k + dot(dscore, qb[n, p, SIDE]))
            more_v.append(near_v + dot(probs, db[n, SIDE, lanes_of(p)]))
        dqkv[1, p] = by_heads(dkey + jnp.concatenate(more_k, axis=0))
        dqkv[2, p] = by_heads(dvalue + jnp.concatenate(more_v, axis=0))
        return carry

    each_pair(key_second)

    dvalues = jnp.concatenate([dqkv[2, p].astype(BF16) for p in range(PAIRS)], axis=1)
    total = partial[...] + dot_nt(dvalues, w[:, pl.ds(2 * WIDTH, WIDTH)])
    total = total + dot_nt(through_norm(1), w[:, pl.ds(WIDTH, WIDTH)])
    out_ref[...] = total.astype(BF16)

    for kind in (0, 1):
        for dr in (-1, 1):

            @pl.when(has(dr, 0))
            def _():
                y_copy(kind, dr).wait_send()

        for dc in (-1, 1):

            @pl.when(has(0, dc))
            def _():
                c_copy(kind, dc).wait_send()

            @pl.when(relays[dc])
            def _():
                from_relay(kind, dc).wait_send()

            for n in (0, 1):

                @pl.when(jnp.logical_and(halo_from(n), has(0, dc)))
                def _():
                    f_copy(kind, n, dc).wait_send()

    for dr, dc in AROUND:

        @pl.when(has(dr, dc))
        def _():
            z_copy(dr, dc).wait_send()


def per_device(grid_input, w_qkv, out_weight, head_scale, cotangent):
    dma = pltpu.SemaphoreType.DMA
    masked = pltpu.VMEM((PAIRS, 2 * OWN, PAIR), BF16)
    by_pair = pltpu.VMEM((PAIRS, GROUP, PAIR), BF16)
    halo_by_pair = pltpu.VMEM((2, PAIRS, 3 * HALF, PAIR), BF16)
    scores = pltpu.VMEM((PAIRS, 2 * OWN, GROUP), F32)
    near_scores = pltpu.VMEM((PAIRS, 2, OWN, HALF), F32)
    side_scores = pltpu.VMEM((PAIRS, 2, OWN, OWN), F32)
    by_query = pltpu.VMEM((PAIRS, 2 * OWN, OWN), F32)
    hbm = pl.BlockSpec(memory_space=pltpu.HBM)
    result = pl.pallas_call(
        kernel,
        out_shape=jax.ShapeDtypeStruct((OWN, D), BF16),
        in_specs=[hbm] * 5,
        out_specs=pl.BlockSpec(memory_space=pltpu.VMEM),
        scratch_shapes=[
            pltpu.SMEM((HEADS,), F32),
            pltpu.VMEM((3, OWN, D), BF16),
            pltpu.VMEM((3, OWN, D), BF16),
            pltpu.VMEM((3, OWN, WIDTH), BF16),
            pltpu.VMEM((2, 3 * HALF, WIDTH), BF16),
            pltpu.VMEM((D, 3 * WIDTH), BF16),
            pltpu.VMEM((D, WIDTH), BF16),
            pltpu.VMEM((OWN, D), BF16),
            *[by_pair] * 3,
            *[halo_by_pair] * 3,
            *[masked] * 4,
            *[pltpu.VMEM((2, OWN, WIDTH), F32)] * 3,
            pltpu.VMEM((2 * OWN, GROUP), F32),
            pltpu.VMEM((2, OWN, HALF), F32),
            pltpu.VMEM((2, OWN, OWN), F32),
            *[scores] * 4,
            *[near_scores] * 4,
            *[side_scores] * 4,
            *[by_query] * 4,
            pltpu.VMEM((2 * HEADS, OWN), F32),
            pltpu.VMEM((9, 2 * HEADS, OWN), F32),
            pltpu.VMEM((2 * HEADS, GROUP), F32),
            pltpu.VMEM((2, 2 * HEADS, HALF), F32),
            pltpu.VMEM((2, 2 * HEADS, OWN), F32),
            pltpu.VMEM((3, PAIRS, OWN, PAIR), F32),
            pltpu.VMEM((OWN, D), F32),
            pltpu.VMEM((OWN, D), BF16),
            pltpu.VMEM((OWN, WIDTH), BF16),
            dma((5,)),
            dma((4,)),
            dma((4,)),
            dma((4,)),
            dma((4,)),
            dma((8,)),
            dma((8,)),
            dma((9,)),
            dma((9,)),
            dma((2,)),
            dma((2,)),
        ],
        compiler_params=pltpu.CompilerParams(
            collective_id=0, has_side_effects=True, vmem_limit_bytes=60 << 20
        ),
    )(
        head_scale,
        grid_input.reshape(OWN, D),
        w_qkv,
        out_weight,
        cotangent.reshape(OWN, D),
    )
    return result.reshape(TILE_H, TILE_W, D)


def solution(mesh):
    placed = (P("row", "col", None), P(), P(), P(), P("row", "col", None))
    return jax.shard_map(
        per_device, mesh=mesh, in_specs=placed, out_specs=P("row", "col", None), check_vma=False
    )
```

```python
import jax
import jax.numpy as jnp
from jax import lax
from jax.experimental import pallas as pl
from jax.experimental.pallas import tpu as pltpu
from jax.sharding import PartitionSpec as P

D = 1024
HEADS = 8
HEAD_DIM = 64
RADIUS = 8
PAIRS = HEADS // 2
PAIR = 2 * HEAD_DIM
WIDTH = HEADS * HEAD_DIM
TILE_H = 16
TILE_W = 8
OWN = TILE_H * TILE_W
RUN = 8
HALF = OWN // 2
GROUP = 3 * OWN

norm_epsilon = 1e-06

MESH = pl.DeviceIdType.MESH
F32 = jnp.float32
BF16 = jnp.bfloat16
AROUND = [(dr, dc) for dr in (-1, 0, 1) for dc in (-1, 0, 1) if (dr, dc) != (0, 0)]


def slot_of(dr, dc):
    return (dr + 1) * 3 + (dc + 1)


def dot(a, b):
    return lax.dot_general(a, b, (((1,), (0,)), ((), ())), preferred_element_type=F32)


def dot_nt(a, b):
    return lax.dot_general(a, b, (((1,), (1,)), ((), ())), preferred_element_type=F32)


def head_sums(array, ones):
    high = array.astype(BF16)
    low = (array - high.astype(F32)).astype(BF16)
    return dot(high, ones) + dot(low, ones)


def kernel(
    scale_hbm, x_hbm, w_hbm, ow_hbm, cot_hbm, out_ref,
    scale_ref, xa, xb, da, db, w, ow, cot,
    qa, ka, va, qb, kb, vb,
    qm, km, vm, dm, raws, back_own, back_raw,
    mask_a, mask_c, mask_s,
    ea, pa, fa, ga, ec, pc, fc, gc, es, ps, fsd, gs,
    zpart, apart, zbc, dbc, zmine, znear, za, zc, zside,
    dqkv, partial, xrelay, drelay,
    local_sem, ys, yr, cs, cr, fs, fr, zs, zr, rs, rr,
):
    nrow, ncol = lax.axis_size("row"), lax.axis_size("col")
    r, c = lax.axis_index("row"), lax.axis_index("col")

    def has(dr, dc):
        ok = None
        for at, d, n in ((r, dr, nrow), (c, dc, ncol)):
            if d:
                here = at > 0 if d < 0 else at < n - 1
                ok = here if ok is None else jnp.logical_and(ok, here)
        return ok

    def device(dr, dc):
        return (jnp.clip(r + dr, 0, nrow - 1), jnp.clip(c + dc, 0, ncol - 1))

    def remote(src, dst, send, recv, dr, dc):
        return pltpu.make_async_remote_copy(
            src_ref=src, dst_ref=dst, send_sem=send, recv_sem=recv,
            device_id=device(dr, dc), device_id_type=MESH,
        )

    place = lax.rem(c, RUN)
    crosses = {
        1: jnp.logical_and(place == RUN - 1, c < ncol - 1),
        -1: jnp.logical_and(place == 0, c > 0),
    }
    relays = {
        1: jnp.logical_and(place == 1, c < ncol - RUN),
        -1: jnp.logical_and(place == RUN - 2, c >= RUN),
    }
    TO_RELAY, FROM_RELAY = -(RUN - 2), RUN - 1

    barrier = pltpu.get_barrier_semaphore()
    count = 0
    for dr, dc in AROUND:
        there = has(dr, dc)
        count = count + there.astype(jnp.int32)

        @pl.when(there)
        def _():
            pl.semaphore_signal(barrier, inc=1, device_id=device(dr, dc), device_id_type=MESH)

    for dc in (-1, 1):
        count = count + crosses[dc].astype(jnp.int32) + relays[dc].astype(jnp.int32)
        for here, to in ((relays[dc], -TO_RELAY * dc), (crosses[-dc], -FROM_RELAY * dc)):

            @pl.when(here)
            def _():
                pl.semaphore_signal(barrier, inc=1, device_id=device(0, to), device_id_type=MESH)

    local = [
        pltpu.make_async_copy(src, dst, local_sem.at[i])
        for i, (src, dst) in enumerate(
            ((cot_hbm, cot), (ow_hbm, ow), (x_hbm, xa.at[0]), (w_hbm, w), (scale_hbm, scale_ref))
        )
    ]
    for copy in local:
        copy.start()

    def block_of(dc):
        return 0 if dc == 0 else (1 if dc < 0 else 2)

    def half(n):
        return pl.ds(HALF * n, HALF)

    def y_copy(kind, dr):
        mine = 0 if dr < 0 else 1
        src, dst = (x_hbm, xb.at[0, half(1 - mine)]) if kind == 0 else (da.at[0], db.at[1 - mine, half(0)])
        i = 2 * kind + (dr > 0)
        return remote(src.at[half(mine)], dst, ys.at[i], yr.at[i], dr, 0)

    def c_copy(kind, dc):
        src, dst = (x_hbm, xa) if kind == 0 else (da.at[0], da)
        i = 2 * kind + (dc > 0)
        return remote(src, dst.at[block_of(-dc)], cs.at[i], cr.at[i], 0, dc)

    def to_relay(kind, dc):
        src, dst = (x_hbm, xrelay) if kind == 0 else (da.at[0], drelay)
        return remote(src, dst, cs.at[2 * kind + (dc > 0)], rr.at[kind], 0, TO_RELAY * dc)

    def from_relay(kind, dc):
        src, dst = (xrelay, xa) if kind == 0 else (drelay, da)
        i = 2 * kind + (dc > 0)
        return remote(src, dst.at[block_of(-dc)], rs.at[kind], cr.at[i], 0, FROM_RELAY * dc)

    def send_own(kind):
        for dc in (-1, 1):

            @pl.when(jnp.logical_and(has(0, dc), jnp.logical_not(crosses[dc])))
            def _():
                c_copy(kind, dc).start()

            @pl.when(crosses[dc])
            def _():
                to_relay(kind, dc).start()

    def relay(kind):
        for dc in (-1, 1):

            @pl.when(relays[dc])
            def _():
                to_relay(kind, dc).wait_recv()
                from_relay(kind, dc).start()

    def f_copy(kind, n, dc):
        i = 4 * kind + 2 * n + (dc > 0)
        b = block_of(-dc)
        if kind == 0:
            src, dst = xb.at[0, half(n)], xb.at[b, half(n)]
        else:
            src, dst = db.at[n, half(0)], db.at[n, half(b)]
        return remote(src, dst, fs.at[i], fr.at[i], 0, dc)

    def z_copy(dr, dc):
        i = slot_of(dr, dc)
        return remote(zmine, znear.at[slot_of(-dr, -dc)], zs.at[i], zr.at[i], dr, dc)

    def halo_from(n):
        return has(-1, 0) if n == 0 else has(1, 0)

    pl.semaphore_wait(barrier, count)
    send_own(0)
    for dr in (-1, 1):

        @pl.when(has(dr, 0))
        def _():
            y_copy(0, dr).start()


    for dc in (-1, 1):

        @pl.when(jnp.logical_not(has(0, dc)))
        def _():
            b = block_of(dc)
            xa[b] = jnp.zeros((OWN, D), BF16)
            da[b] = jnp.zeros((OWN, WIDTH), BF16)
            xb[b] = jnp.zeros((OWN, D), BF16)
            for n in (0, 1):
                db[n, half(b)] = jnp.zeros((HALF, WIDTH), BF16)

    for n in (0, 1):

        @pl.when(jnp.logical_not(halo_from(n)))
        def _():
            for b in range(3):
                xb[b, half(n)] = jnp.zeros((HALF, D), BF16)
            db[n] = jnp.zeros((3 * HALF, WIDTH), BF16)

    for dr, dc in AROUND:

        @pl.when(jnp.logical_not(has(dr, dc)))
        def _():
            znear[slot_of(dr, dc)] = jnp.zeros((2 * HEADS, OWN), F32)

    local[0].wait()
    local[1].wait()
    for n in range(2):
        cols = pl.ds(256 * n, 256)
        da[0, :, cols] = dot(cot[...], ow[:, cols]).astype(BF16)
    send_own(1)

    local[4].wait()
    local[2].wait()
    local[3].wait()

    def head_ones(n):
        a = lax.broadcasted_iota(jnp.int32, (n, n), 0) // HEAD_DIM
        b = lax.broadcasted_iota(jnp.int32, (n, n), 1) // HEAD_DIM
        return jnp.where(a == b, 1.0, 0.0).astype(BF16)

    def scale_row(first, heads):
        lane = lax.broadcasted_iota(jnp.int32, (1, heads * HEAD_DIM), 1) // HEAD_DIM
        row = jnp.zeros((1, heads * HEAD_DIM), F32)
        for h in range(heads):
            row = jnp.where(lane == h, scale_ref[first + h], row)
        return jnp.sqrt(row)

    quad_rows = [scale_row(0, 4), scale_row(4, 4)]
    ones256 = head_ones(256)

    def window(rows, first_half, lanes, block, halo, first_block):
        row = lax.broadcasted_iota(jnp.int32, (rows, lanes), 0)
        lane = lax.broadcasted_iota(jnp.int32, (rows, lanes), 1)
        own_i = (row // OWN + first_half) * RADIUS + (row % HALF) // TILE_W
        own_j = row % TILE_W
        b = lane // block + first_block
        there_i = (lane % block) // TILE_W
        if halo:
            there_i = there_i - RADIUS if first_half == 0 else there_i + TILE_H
        there_j = lane % TILE_W + jnp.where(b == 0, 0, jnp.where(b == 1, -TILE_W, TILE_W))
        row_at, col_at = r * TILE_H + there_i, c * TILE_W + there_j
        near = (jnp.abs(there_i - own_i) <= RADIUS) & (jnp.abs(there_j - own_j) <= RADIUS)
        inside = (row_at >= 0) & (row_at < nrow * TILE_H) & (col_at >= 0) & (col_at < ncol * TILE_W)
        return jnp.where(near & inside, 1.0, 0.0)

    mask_a[...] = window(2 * OWN, 0, GROUP, OWN, False, 0)
    for n in (0, 1):
        mask_c[n] = window(OWN, n, HALF, HALF, True, 0)
        mask_s[n] = window(OWN, n, OWN, HALF, True, 1)

    relay(0)

    def project(x_rows, store, own=False, chunks=range(6)):
        for n in chunks:
            values = dot(x_rows, w[:, pl.ds(256 * n, 256)])
            kind, quad = n // 2, n % 2
            if kind < 2:
                if own:
                    squares = head_sums(values * values, ones256) + norm_epsilon
                    factor = quad_rows[quad] * lax.rsqrt(squares)
                    cols = pl.ds(256 * quad, 256)
                    raws[kind, :, cols] = values
                    back_own[kind, :, cols] = factor
                    back_raw[kind, :, cols] = factor * values / squares
                else:
                    squares = head_sums(values * values, ones256) + norm_epsilon
                    factor = quad_rows[quad] * lax.rsqrt(squares)
                values = values * factor
            result = values.astype(BF16)
            store(kind, 2 * quad, result[:, :PAIR])
            store(kind, 2 * quad + 1, result[:, PAIR:])

    def store_a(first):
        def store(kind, p, result):
            (qa, ka, va)[kind][p, pl.ds(first, result.shape[0])] = result

        return store

    def store_b(first):
        def store(kind, p, result):
            to = (qb, kb, vb)[kind]
            for i in range(result.shape[0] // HALF):
                to[i % 2, p, half(first + i // 2)] = result[HALF * i : HALF * (i + 1)]

        return store

    project(xa[0], store_a(0), own=True)
    for dr in (-1, 1):

        @pl.when(has(dr, 0))
        def _():
            y_copy(1, dr).start()

    first_lanes = lax.broadcasted_iota(jnp.int32, (HALF, PAIR), 1) < HEAD_DIM
    zero = jnp.zeros((HALF, PAIR), BF16)
    for p in range(PAIRS):
        for to, values in (
            (qm, qa[p, pl.ds(0, OWN)]), (km, ka[p, pl.ds(0, OWN)]), (vm, va[p, pl.ds(0, OWN)]),
            (dm, da[0, :, pl.ds(PAIR * p, PAIR)]),
        ):
            for n in (0, 1):
                rows = values[HALF * n : HALF * (n + 1)]
                to[p, half(2 * n)] = jnp.where(first_lanes, rows, zero)
                to[p, half(2 * n + 1)] = jnp.where(first_lanes, zero, rows)

    def pass_on(kind):
        for n, dr in ((0, 1), (1, -1)):

            @pl.when(halo_from(n))
            def _():
                y_copy(kind, dr).wait_recv()
                for dc in (-1, 1):

                    @pl.when(has(0, dc))
                    def _():
                        f_copy(kind, n, dc).start()

    def corners(kind):
        for n in (0, 1):
            for dc in (-1, 1):

                @pl.when(jnp.logical_and(halo_from(n), has(0, -dc)))
                def _():
                    f_copy(kind, n, dc).wait_recv()

    def lanes_of(p):
        return pl.ds(pl.multiple_of(p * PAIR, PAIR), PAIR)

    NEAR, SIDE = pl.ds(0, HALF), pl.ds(HALF, OWN)

    def rows_of(n):
        return pl.ds(OWN * n, OWN)

    def each_pair(body):
        lax.fori_loop(0, PAIRS, body, 0, unroll=True)

    pass_on(0)
    project(xb[0], store_b(0))

    def near_scores(p, carry):
        z, along = [], []
        for n in (0, 1):
            e = jnp.exp(dot_nt(qm[p, rows_of(n)], kb[n, p, NEAR])) * mask_c[n]
            dp = dot_nt(dm[p, rows_of(n)], vb[n, p, NEAR])
            ec[p, n] = e
            pc[p, n] = dp
            fc[p, n] = jnp.exp(dot_nt(km[p, rows_of(n)], qb[n, p, NEAR])) * mask_c[n]
            z.append(e)
            along.append(e * dp)
        rest = jnp.zeros((2 * OWN, HALF), F32)
        zpart[p] = jnp.concatenate([jnp.concatenate(z, axis=0), rest], axis=1)
        apart[p] = jnp.concatenate([jnp.concatenate(along, axis=0), rest], axis=1)
        return carry

    each_pair(near_scores)

    relay(1)
    for dc in (-1, 1):

        @pl.when(has(0, -dc))
        def _():
            c_copy(0, dc).wait_recv()

    project(xa[1:3].reshape(2 * OWN, D), store_a(OWN))

    def tiles(array):
        return array[:, :OWN] + array[:, OWN : 2 * OWN] + array[:, 2 * OWN :]

    def query_a(p, carry):
        e = jnp.exp(dot_nt(qm[p], ka[p])) * mask_a[...]
        dp = dot_nt(dm[p], va[p])
        ea[p] = e
        pa[p] = dp
        zpart[p] = zpart[p] + tiles(e)
        apart[p] = apart[p] + tiles(e * dp)
        return carry

    lax.fori_loop(0, PAIRS, query_a, 0, unroll=True)

    corners(0)
    x_sides = xb[1:3].reshape(2 * OWN, D)
    project(x_sides, store_b(1), chunks=range(2, 6))

    lane = lax.broadcasted_iota(jnp.int32, (2 * OWN, OWN), 1)

    def side_scores(p, table):
        z, along = [], []
        for n in (0, 1):
            e = jnp.exp(dot_nt(qm[p, rows_of(n)], kb[n, p, SIDE])) * mask_s[n]
            dp = dot_nt(dm[p, rows_of(n)], vb[n, p, SIDE])
            es[p, n] = e
            ps[p, n] = dp
            z.append(e)
            along.append(e * dp)
        z = jnp.sum(jnp.concatenate(z, axis=0) + zpart[p], axis=1, keepdims=True)
        along = jnp.sum(jnp.concatenate(along, axis=0) + apart[p], axis=1, keepdims=True)
        inverse = 1.0 / z
        delta = along * inverse
        zbc[p] = jnp.broadcast_to(inverse, (2 * OWN, OWN))
        dbc[p] = jnp.broadcast_to(delta, (2 * OWN, OWN))
        table = jnp.where(lane == p, inverse, table)
        return jnp.where(lane == PAIRS + p, delta, table)

    table = lax.fori_loop(0, PAIRS, side_scores, jnp.zeros((2 * OWN, OWN), F32), unroll=True)
    upper, lower = table[:OWN].T[:HEADS], table[OWN:].T[:HEADS]
    left_lanes = lax.broadcasted_iota(jnp.int32, (HEADS, OWN), 1) < HALF
    zmine[pl.ds(0, HEADS)] = jnp.where(left_lanes, upper, pltpu.roll(lower, HALF, 1))
    zmine[pl.ds(HEADS, HEADS)] = jnp.where(left_lanes, pltpu.roll(upper, HALF, 1), lower)
    for dr, dc in AROUND:

        @pl.when(has(dr, dc))
        def _():
            z_copy(dr, dc).start()

    pass_on(1)

    project(x_sides, store_b(1), chunks=range(2))

    def key_sides(p, carry):
        for n in (0, 1):
            fsd[p, n] = jnp.exp(dot_nt(km[p, rows_of(n)], qb[n, p, SIDE])) * mask_s[n]
        return carry

    each_pair(key_sides)

    for dc in (-1, 1):

        @pl.when(has(0, -dc))
        def _():
            c_copy(1, dc).wait_recv()

    def key_a(p, carry):
        fa[p] = jnp.exp(dot_nt(km[p], qa[p])) * mask_a[...]
        ga[p] = dot_nt(vm[p], da[:, :, lanes_of(p)].reshape(GROUP, PAIR))
        return carry

    each_pair(key_a)

    def by_heads(array):
        parts = [array[HALF * i : HALF * (i + 1)] for i in range(4)]
        return jnp.concatenate(
            [jnp.where(first_lanes, parts[2 * n], parts[2 * n + 1]) for n in (0, 1)], axis=0
        )

    def query_second(p, carry):
        inverse, delta = zbc[p], dbc[p]
        wide = jnp.concatenate([inverse] * 3, axis=1)
        dscore = ea[p] * wide * (pa[p] - jnp.concatenate([delta] * 3, axis=1))
        result = dot(dscore.astype(BF16), ka[p])
        more = []
        for n in (0, 1):
            rows = slice(OWN * n, OWN * (n + 1))
            dscore = ec[p, n] * inverse[rows, :HALF] * (pc[p, n] - delta[rows, :HALF])
            near = dot(dscore.astype(BF16), kb[n, p, NEAR])
            dscore = es[p, n] * inverse[rows] * (ps[p, n] - delta[rows])
            more.append(near + dot(dscore.astype(BF16), kb[n, p, SIDE]))
        dqkv[0, p] = by_heads(result + jnp.concatenate(more, axis=0))
        return carry

    each_pair(query_second)
    ones128 = head_ones(PAIR)

    def through_norm(kind):
        blocks = []
        for p in range(PAIRS):
            grads = dqkv[kind, p]
            cols = pl.ds(PAIR * p, PAIR)
            along = head_sums(grads * raws[kind, :, cols], ones128)
            blocks.append(
                (back_own[kind, :, cols] * grads - back_raw[kind, :, cols] * along).astype(BF16)
            )
        return jnp.concatenate(blocks, axis=1)

    partial[...] = dot_nt(through_norm(0), w[:, pl.ds(0, WIDTH)])

    corners(1)

    def key_halo_cot(p, carry):
        for n in (0, 1):
            gc[p, n] = dot_nt(vm[p, rows_of(n)], db[n, NEAR, lanes_of(p)])
            gs[p, n] = dot_nt(vm[p, rows_of(n)], db[n, SIDE, lanes_of(p)])
        return carry

    each_pair(key_halo_cot)

    for dr, dc in AROUND:

        @pl.when(has(dr, dc))
        def _():
            z_copy(-dr, -dc).wait_recv()

    znear[slot_of(0, 0)] = zmine[...]
    near_lanes = lax.broadcasted_iota(jnp.int32, (2 * HEADS, OWN), 1) < HALF
    for b, dc in enumerate((0, -1, 1)):
        za[:, pl.ds(b * OWN, OWN)] = znear[slot_of(0, dc)]
    own_up, left_up, right_up = (znear[slot_of(-1, dc)] for dc in (0, -1, 1))
    zc[0] = pltpu.roll(own_up, HALF, 1)[:, :HALF]
    zside[0] = jnp.where(near_lanes, pltpu.roll(left_up, HALF, 1), right_up)
    own_down, left_down, right_down = (znear[slot_of(1, dc)] for dc in (0, -1, 1))
    zc[1] = own_down[:, :HALF]
    zside[1] = jnp.where(near_lanes, left_down, pltpu.roll(right_down, HALF, 1))

    def terms(e, dp, table, p, halves):
        probs, dscore = [], []
        for i in range(2 * halves):
            rows = slice(HALF * i, HALF * (i + 1))
            first = HEADS * (i % 2)
            prob = e[rows] * table[pl.ds(first + p, 1), :]
            probs.append(prob.astype(BF16))
            dscore.append((prob * (dp[rows] - table[pl.ds(first + PAIRS + p, 1), :])).astype(BF16))
        return jnp.concatenate(probs, axis=0), jnp.concatenate(dscore, axis=0)

    def key_second(p, carry):
        probs, dscore = terms(fa[p], ga[p], za, p, 2)
        dkey = dot(dscore, qa[p])
        dvalue = dot(probs, da[:, :, lanes_of(p)].reshape(GROUP, PAIR))
        more_k, more_v = [], []
        for n in (0, 1):
            probs, dscore = terms(fc[p, n], gc[p, n], zc.at[n], p, 1)
            near_k = dot(dscore, qb[n, p, NEAR])
            near_v = dot(probs, db[n, NEAR, lanes_of(p)])
            probs, dscore = terms(fsd[p, n], gs[p, n], zside.at[n], p, 1)
            more_k.append(near_k + dot(dscore, qb[n, p, SIDE]))
            more_v.append(near_v + dot(probs, db[n, SIDE, lanes_of(p)]))
        dqkv[1, p] = by_heads(dkey + jnp.concatenate(more_k, axis=0))
        dqkv[2, p] = by_heads(dvalue + jnp.concatenate(more_v, axis=0))
        return carry

    each_pair(key_second)

    dvalues = jnp.concatenate([dqkv[2, p].astype(BF16) for p in range(PAIRS)], axis=1)
    total = partial[...] + dot_nt(dvalues, w[:, pl.ds(2 * WIDTH, WIDTH)])
    total = total + dot_nt(through_norm(1), w[:, pl.ds(WIDTH, WIDTH)])
    out_ref[...] = total.astype(BF16)

    for kind in (0, 1):
        for dr in (-1, 1):

            @pl.when(has(dr, 0))
            def _():
                y_copy(kind, dr).wait_send()

        for dc in (-1, 1):

            @pl.when(has(0, dc))
            def _():
                c_copy(kind, dc).wait_send()

            @pl.when(relays[dc])
            def _():
                from_relay(kind, dc).wait_send()

            for n in (0, 1):

                @pl.when(jnp.logical_and(halo_from(n), has(0, dc)))
                def _():
                    f_copy(kind, n, dc).wait_send()

    for dr, dc in AROUND:

        @pl.when(has(dr, dc))
        def _():
            z_copy(dr, dc).wait_send()


def per_device(grid_input, w_qkv, out_weight, head_scale, cotangent):
    dma = pltpu.SemaphoreType.DMA
    masked = pltpu.VMEM((PAIRS, 2 * OWN, PAIR), BF16)
    by_pair = pltpu.VMEM((PAIRS, GROUP, PAIR), BF16)
    halo_by_pair = pltpu.VMEM((2, PAIRS, 3 * HALF, PAIR), BF16)
    scores = pltpu.VMEM((PAIRS, 2 * OWN, GROUP), F32)
    near_scores = pltpu.VMEM((PAIRS, 2, OWN, HALF), F32)
    side_scores = pltpu.VMEM((PAIRS, 2, OWN, OWN), F32)
    by_query = pltpu.VMEM((PAIRS, 2 * OWN, OWN), F32)
    hbm = pl.BlockSpec(memory_space=pltpu.HBM)
    result = pl.pallas_call(
        kernel,
        out_shape=jax.ShapeDtypeStruct((OWN, D), BF16),
        in_specs=[hbm] * 5,
        out_specs=pl.BlockSpec(memory_space=pltpu.VMEM),
        scratch_shapes=[
            pltpu.SMEM((HEADS,), F32),
            pltpu.VMEM((3, OWN, D), BF16),
            pltpu.VMEM((3, OWN, D), BF16),
            pltpu.VMEM((3, OWN, WIDTH), BF16),
            pltpu.VMEM((2, 3 * HALF, WIDTH), BF16),
            pltpu.VMEM((D, 3 * WIDTH), BF16),
            pltpu.VMEM((D, WIDTH), BF16),
            pltpu.VMEM((OWN, D), BF16),
            *[by_pair] * 3,
            *[halo_by_pair] * 3,
            *[masked] * 4,
            *[pltpu.VMEM((2, OWN, WIDTH), F32)] * 3,
            pltpu.VMEM((2 * OWN, GROUP), F32),
            pltpu.VMEM((2, OWN, HALF), F32),
            pltpu.VMEM((2, OWN, OWN), F32),
            *[scores] * 4,
            *[near_scores] * 4,
            *[side_scores] * 4,
            *[by_query] * 4,
            pltpu.VMEM((2 * HEADS, OWN), F32),
            pltpu.VMEM((9, 2 * HEADS, OWN), F32),
            pltpu.VMEM((2 * HEADS, GROUP), F32),
            pltpu.VMEM((2, 2 * HEADS, HALF), F32),
            pltpu.VMEM((2, 2 * HEADS, OWN), F32),
            pltpu.VMEM((3, PAIRS, OWN, PAIR), F32),
            pltpu.VMEM((OWN, D), F32),
            pltpu.VMEM((OWN, D), BF16),
            pltpu.VMEM((OWN, WIDTH), BF16),
            dma((5,)),
            dma((4,)),
            dma((4,)),
            dma((4,)),
            dma((4,)),
            dma((8,)),
            dma((8,)),
            dma((9,)),
            dma((9,)),
            dma((2,)),
            dma((2,)),
        ],
        compiler_params=pltpu.CompilerParams(
            collective_id=0, has_side_effects=True, vmem_limit_bytes=60 << 20
        ),
    )(
        head_scale,
        grid_input.reshape(OWN, D),
        w_qkv,
        out_weight,
        cotangent.reshape(OWN, D),
    )
    return result.reshape(TILE_H, TILE_W, D)


def solution(mesh):
    placed = (P("row", "col", None), P(), P(), P(), P("row", "col", None))
    return jax.shard_map(
        per_device, mesh=mesh, in_specs=placed, out_specs=P("row", "col", None), check_vma=False
    )
```
